1024 devices in a mesh: dp: 2 (over core), expert: 64 (over y, z), tensor: 8 (over x).
Axes of the slice: x: 8, y: 8, z: 8, core: 2. Of those that a mesh axis runs over, the one named last changes fastest.
Arguments:
- grad_out: bfloat16 [4096, 3584], P(('dp', 'expert', 'tensor')), parts along dimension 0, may hold values from -6 to 6
- routes: int32 [4096, 2], P(('dp', 'expert')), parts along dimension 0, may hold values from 0 to 63, all different within a row; in each aligned block of 32 rows (0 to 31, 32 to 63, ...) at most 2 rows name the same one
- gate_probs: bfloat16 [4096, 2], P(('dp', 'expert')), parts along dimension 0, may hold values from 0.099609375 to 0.8984375
- dense_gate_pre: bfloat16 [4096, 2432], P(('dp', 'expert'), 'tensor'), parts along dimension 0, may hold values from -6 to 6
- dense_up_pre: bfloat16 [4096, 2432], P(('dp', 'expert'), 'tensor'), parts along dimension 0, may hold values from -6 to 6
- dense_w_gate: bfloat16 [3584, 2432], P('expert', 'tensor'), may hold values from -0.125 to 0.125
- dense_w_up: bfloat16 [3584, 2432], P('expert', 'tensor'), may hold values from -0.125 to 0.125
- dense_w_down: bfloat16 [2432, 3584], P('tensor'), may hold values from -0.09375 to 0.09375
- expert_gate_pre: bfloat16 [128, 128, 2432], P(('dp', 'expert'), None, 'tensor'), parts along dimension 0, may hold values from -6 to 6
- expert_up_pre: bfloat16 [128, 128, 2432], P(('dp', 'expert'), None, 'tensor'), parts along dimension 0, may hold values from -6 to 6
- expert_w_gate: bfloat16 [64, 3584, 2432], P('expert', None, 'tensor'), may hold values from -0.125 to 0.125
- expert_w_up: bfloat16 [64, 3584, 2432], P('expert', None, 'tensor'), may hold values from -0.125 to 0.125
- expert_w_down: bfloat16 [64, 2432, 3584], P('expert', 'tensor'), may hold values from -0.09375 to 0.09375
Outputs:
- grad_in: bfloat16 [4096, 3584], P(('dp', 'expert', 'tensor')), parts along dimension 0
The draws below stay inside these ranges and needn't reach their ends.
There are 2 independent parts, one for each index of `dp`. The reference program is written for one: setup_inputs(seed, part) draws one part's arguments, and reference() takes and returns one part's arrays. A program takes and returns all parts, laid end to end along the dimension named above; an argument that names none is the same for every part. Nothing has to cross between parts.
Inputs may be any that keep to these rules, and one draw needn't show every extreme that they name: `routes`: each token names two different experts. Within each token group of 32 tokens no expert is named by more than 2 tokens, a bound that some block reaches.
All inputs are finite; a program needn't handle non-finite values.
Results may differ from the reference program's by a relative error of at most 0.017.
Values may be sent and summed in bfloat16 or wider, within the bound.
A program may use at most 64 MiB of HBM per device.

```python
import math
import jax
import jax.numpy as jnp
import numpy as np
from jax import lax

D = 3584
FD = 2432
FE = 2432
TOK_DEV = 4
EXPERTS = 64
TOKENS = 2048
CAP = 2
SLOTS = 128
N_EXPERT = 64
N_TENSOR = 8


def levels(stream_key, shape, cuts, low, high):
    level = 1.0
    for axis_at, blocks in cuts:
        steps = jax.random.uniform(jax.random.fold_in(jax.random.fold_in(stream_key, 6), axis_at), (blocks,), jnp.float32, low / len(cuts), high / len(cuts))
        level = level * jnp.repeat(jnp.exp(steps), shape[axis_at] // blocks).reshape((-1,) + (1,) * (len(shape) - 1 - axis_at))
    return level


def assign_block(key, own, number, rows, amount, top, bound, slope):
    order = jax.random.permutation(key, amount)
    crowded, common = portions_of(amount, rows * top, bound, slope, True), portions_of(amount, rows * top, bound, slope, False)
    places = jnp.arange(amount)

    def named(lengths, rotation):
        used = int((lengths > 0).sum())
        fixed = max(1, used // 4)
        shifted = fixed + (places - fixed + rotation * (used - fixed)) % max(1, amount - fixed)
        return jnp.zeros((amount,), jnp.int32).at[order[jnp.where(places < fixed, places, shifted)]].set(jnp.asarray(lengths, jnp.int32))

    lengths = jnp.where(number % 4 == 0, named(crowded, number // 4), named(common, number - number // 4 - 1))
    mixed = jax.random.permutation(jax.random.fold_in(own, 3), amount)
    source_of, sink = mixed[0:amount // 2 * 2:2], mixed[1:amount // 2 * 2:2]
    slack = jnp.minimum(lengths[source_of] - 1, bound - lengths[sink]) // 2
    slack = jnp.where((source_of == order[0]) | (sink == order[0]) | (lengths[sink] == 0), 0, jnp.maximum(slack, 0))
    shifted = jax.random.randint(jax.random.fold_in(own, 4), (amount // 2,), 0, 1 << 20) % (slack + 1)
    lengths = lengths.at[source_of].add(-shifted).at[sink].add(shifted)
    items = jnp.searchsorted(jnp.cumsum(lengths), jnp.arange(rows * top), side="right").astype(jnp.int32)
    listing = items.reshape(top, rows).T
    listing = listing[jax.random.permutation(jax.random.fold_in(own, 1), rows)]
    rotation = jax.random.randint(jax.random.fold_in(own, 2), (rows, 1), 0, top)
    return jnp.take_along_axis(listing, (jnp.arange(top)[None, :] + rotation) % top, axis=1)


def portions_of(amount, total, bound, lean, full):
    weights = [(1 << 20) // math.isqrt(standing ** lean) + 1 for standing in range(1, amount + 1)]
    largest = bound if full else min(bound, max(-(-total // amount), total * weights[0] // sum(weights)))
    least = 1 if total - largest >= amount - 1 else 0
    holding, rest = [largest] + [least] * (amount - 1), total - largest - least * (amount - 1)
    while rest > 0:
        movable = [i for i in range(1, amount) if holding[i] < largest] or [i for i in range(1, amount) if holding[i] < bound]
        pool, left = sum([weights[i] for i in movable]), rest
        for i in movable:
            extra = min(bound - holding[i], max(1, left * weights[i] // pool), rest)
            holding[i] = holding[i] + extra
            rest = rest - extra
    return np.array(holding)


def noise(own_key, extent, deviation, reach, cuts=(), held_as=jnp.bfloat16):
    loudness = levels(own_key, extent, cuts, -0.22, 0.18) if cuts else 1.0
    drawn = jax.random.normal(own_key, extent, jnp.float32) * deviation * loudness
    return jnp.minimum(jnp.maximum(drawn, -reach), reach).astype(held_as)


def setup_inputs(seed: int = 0, part: int = 0) -> dict:
    splits = jax.random.split(jax.random.key(seed), 14)
    own_keys = jax.random.split(jax.random.fold_in(splits[13], part), 14)
    grad_out = noise(own_keys[0], (TOKENS, D), 1.0, 6.0, ((0, 512),))
    routes_keys = jax.random.split(jax.random.fold_in(own_keys[1], 1), TOKENS // (TOK_DEV * N_TENSOR))
    routes_turns = jax.random.permutation(jax.random.fold_in(own_keys[1], 3), TOKENS // (TOK_DEV * N_TENSOR))
    routes = jax.vmap(lambda own, number: assign_block(jax.random.fold_in(own_keys[1], 2), own, number, TOK_DEV * N_TENSOR, EXPERTS, 2, CAP, 1))(routes_keys, routes_turns).reshape((TOKENS, 2))
    gate_probs = jnp.clip(0.099609375 + 0.7988281 * jax.random.uniform(own_keys[2], (TOKENS, 2), jnp.float32) ** levels(own_keys[2], (TOKENS, 2), ((0, 64),), -0.2, 0.2), 0.099609375, 0.8984375).astype(jnp.bfloat16)
    dense_gate_pre = noise(own_keys[3], (TOKENS, FD), 1.5, 6.0, ((0, 64), (1, 8)))
    dense_up_pre = noise(own_keys[4], (TOKENS, FD), 1.0, 6.0, ((0, 64), (1, 8)))
    dense_w_gate = noise(splits[5], (D, FD), FD ** -0.5, 0.125, ((0, 64), (1, 8)))
    dense_w_up = noise(splits[6], (D, FD), FD ** -0.5, 0.125, ((0, 64), (1, 8)))
    dense_w_down = noise(splits[7], (FD, D), D ** -0.5, 0.09375, ((0, 8),))
    expert_gate_pre = noise(own_keys[8], (EXPERTS, SLOTS, FE), 1.5, 6.0, ((0, 64), (2, 8)))
    expert_up_pre = noise(own_keys[9], (EXPERTS, SLOTS, FE), 1.0, 6.0, ((0, 64), (2, 8)))
    expert_w_gate = noise(splits[10], (EXPERTS, D, FE), FE ** -0.5, 0.125, ((0, 64), (2, 8)))
    expert_w_up = noise(splits[11], (EXPERTS, D, FE), FE ** -0.5, 0.125, ((0, 64), (2, 8)))
    expert_w_down = noise(splits[12], (EXPERTS, FE, D), D ** -0.5, 0.09375, ((0, 64), (1, 8)))
    return dict(grad_out=grad_out, routes=routes, gate_probs=gate_probs, dense_gate_pre=dense_gate_pre, dense_up_pre=dense_up_pre, dense_w_gate=dense_w_gate, dense_w_up=dense_w_up, dense_w_down=dense_w_down, expert_gate_pre=expert_gate_pre, expert_up_pre=expert_up_pre, expert_w_gate=expert_w_gate, expert_w_up=expert_w_up, expert_w_down=expert_w_down)


def swiglu_back(upstream, gate_pre, up_pre):
    gate_value = gate_pre.astype(jnp.float32)
    up_value = up_pre.astype(jnp.float32)
    sigmoid_gate = jax.nn.sigmoid(gate_value)
    silu_value = gate_value * sigmoid_gate
    silu_slope = sigmoid_gate * (1.0 + gate_value * (1.0 - sigmoid_gate))
    grad_gate = (upstream * up_value * silu_slope).astype(jnp.bfloat16)
    grad_up = (upstream * silu_value).astype(jnp.bfloat16)
    return grad_gate, grad_up


def reference(grad_out, routes, gate_probs, dense_gate_pre, dense_up_pre, dense_w_gate, dense_w_up, dense_w_down, expert_gate_pre, expert_up_pre, expert_w_gate, expert_w_up, expert_w_down):
    group_size = TOK_DEV * N_TENSOR
    upstream = jnp.dot(grad_out, dense_w_down.T, preferred_element_type=jnp.float32)
    dense_gg, dense_gu = swiglu_back(upstream, dense_gate_pre, dense_up_pre)
    pair_expert = routes.reshape(N_EXPERT, 2 * group_size)
    expert_ids = jnp.arange(EXPERTS, dtype=jnp.int32)
    expert_hits = (pair_expert[:, :, None] == expert_ids[None, None, :]).astype(jnp.int32)
    earlier = jnp.cumsum(expert_hits, axis=1) - expert_hits
    slot_index = jnp.sum(earlier * expert_hits, axis=2).astype(jnp.int32)
    group_ids = jnp.arange(N_EXPERT, dtype=jnp.int32)[:, None]
    targets = (pair_expert * SLOTS + group_ids * CAP + slot_index).reshape(-1).astype(jnp.int32)
    buffers = jnp.zeros((EXPERTS * SLOTS, D), jnp.bfloat16)
    buffers = buffers.at[targets].set(jnp.repeat(grad_out, 2, axis=0)).reshape(EXPERTS, SLOTS, D)

    def expert_grads(items):
        slot_rows, gate_pre, up_pre, w_down = items
        ups = jnp.dot(slot_rows, w_down.T, preferred_element_type=jnp.float32)
        return swiglu_back(ups, gate_pre, up_pre)

    expert_gg, expert_gu = lax.map(expert_grads, (buffers, expert_gate_pre, expert_up_pre, expert_w_down))
    probs = gate_probs.astype(jnp.float32)
    dense_width = FD // N_TENSOR
    expert_width = FE // N_TENSOR
    summed = jnp.zeros((TOKENS, D), jnp.float32)
    for member in range(N_TENSOR):
        dense_low = member * dense_width
        dense_high = dense_low + dense_width
        expert_low = member * expert_width
        expert_high = expert_low + expert_width
        dense_part = jnp.dot(dense_gg[:, dense_low:dense_high], dense_w_gate[:, dense_low:dense_high].T, preferred_element_type=jnp.float32)
        dense_part = dense_part + jnp.dot(dense_gu[:, dense_low:dense_high], dense_w_up[:, dense_low:dense_high].T, preferred_element_type=jnp.float32)

        def expert_back(items, expert_low=expert_low, expert_high=expert_high):
            grad_gate, grad_up, w_gate, w_up = items
            result = jnp.dot(grad_gate[:, expert_low:expert_high], w_gate[:, expert_low:expert_high].T, preferred_element_type=jnp.float32)
            result = result + jnp.dot(grad_up[:, expert_low:expert_high], w_up[:, expert_low:expert_high].T, preferred_element_type=jnp.float32)
            return result.astype(jnp.bfloat16)

        returned = lax.map(expert_back, (expert_gg, expert_gu, expert_w_gate, expert_w_up))
        returned = lax.optimization_barrier(returned.reshape(EXPERTS * SLOTS, D))
        picked = returned[targets].astype(jnp.float32).reshape(TOKENS, 2, D)
        routed_part = jnp.sum(probs[:, :, None] * picked, axis=1)
        rounded = lax.optimization_barrier((dense_part + routed_part).astype(jnp.bfloat16))
        summed = summed + rounded.astype(jnp.float32)
    return (grad_out.astype(jnp.float32) + summed).astype(jnp.bfloat16)
```

```python
import functools
import math

import jax
import jax.numpy as jnp
from jax import lax
from jax.experimental import pallas as pl
from jax.experimental.pallas import tpu as pltpu
from jax.sharding import PartitionSpec as P

BF = jnp.bfloat16
F32 = jnp.float32
NT = (((1,), (1,)), ((), ()))
TN = (((0,), (0,)), ((), ()))
NN = (((1,), (0,)), ((), ()))


def mod(value, n):
    return lax.rem(value + 4 * n, n)


def dot(a, b, dims):
    return lax.dot_general(a, b, dims, preferred_element_type=F32)


def swiglu_back(upstream, gate_pre, up_pre):
    gate = gate_pre.astype(F32)
    up = up_pre.astype(F32)
    sigma = 1.0 / (1.0 + jnp.exp(-gate))
    grad_gate = upstream * up * (sigma * (1.0 + gate * (1.0 - sigma)))
    grad_up = upstream * (gate * sigma)
    return grad_gate.astype(BF), grad_up.astype(BF)


def kernel(
    NX, NY, NZ, C,
    grad, routes, probs, dgp, dup, dwg, dwu, dwd, egp, eup, ewg, ewu, ewd,
    out,
    xg, xf, xb, rt, pr, dgp_v, dup_v, dwd_v, egp_v, eup_v, ewd_v, ewg_v, ewu_v,
    wg, wf, gg, do_s, do_r, rf, s2, r2, s6, r6, ag, bk, rr, rs, s8, r8, tot,
    ld_sem, p1_s, p1_r, wz_s, wz_r, sib, gg_s, gg_r, do_ss, do_rs,
    p2_s, p2_r, p6_s, p6_r, ag_s, ag_r, rs_s, rs_r, p8_s, p8_r,
):
    T, D = grad.shape
    G = NX * T
    F = dwd.shape[0]
    RB = ag.shape[1]
    CW = D // C
    DB = do_s.shape[2]
    DR = dwg.shape[0]
    SL = NY * RB

    dp = lax.axis_index("dp")
    ex = lax.axis_index("expert")
    m = lax.axis_index("tensor")
    y = ex // NZ
    z = ex % NZ

    def rcopy(src, dst, ss, rsem, device):
        return pltpu.make_async_remote_copy(
            src_ref=src, dst_ref=dst, send_sem=ss, recv_sem=rsem,
            device_id=device, device_id_type=pl.DeviceIdType.MESH,
        )

    def at_x(x):
        return (dp, ex, x)

    def at_yz(yy, zz):
        return (dp, yy * NZ + zz, m)

    sibling = (1 - dp, ex, m)
    own_pair = mod(m + z, NY) == 0
    other_pair = jnp.logical_not(own_pair)

    loads = [
        pltpu.make_async_copy(grad, xg.at[m], ld_sem.at[0]),
        pltpu.make_async_copy(routes, rt, ld_sem.at[1]),
        pltpu.make_async_copy(probs, pr, ld_sem.at[2]),
        pltpu.make_async_copy(dwd, dwd_v, ld_sem.at[3]),
        pltpu.make_async_copy(dgp, dgp_v, ld_sem.at[4]),
        pltpu.make_async_copy(dup, dup_v, ld_sem.at[5]),
        pltpu.make_async_copy(ewd.at[0], ewd_v, ld_sem.at[6]),
        pltpu.make_async_copy(egp.at[0], egp_v, ld_sem.at[7]),
        pltpu.make_async_copy(eup.at[0], eup_v, ld_sem.at[8]),
        pltpu.make_async_copy(ewg.at[0], ewg_v, ld_sem.at[9]),
        pltpu.make_async_copy(ewu.at[0], ewu_v, ld_sem.at[10]),
    ]
    own_gate = pltpu.make_async_copy(dwg, wg.at[0, z], ld_sem.at[11])
    own_up = pltpu.make_async_copy(dwu, wg.at[1, z], ld_sem.at[11])

    @pl.when(dp == 0)
    def _():
        own_gate.start()

    @pl.when(dp == 1)
    def _():
        own_up.start()

    for load in loads:
        load.start()

    barrier = pltpu.get_barrier_semaphore()

    def greet(device):
        pl.semaphore_signal(barrier, inc=1, device_id=device, device_id_type=pl.DeviceIdType.MESH)

    for k in range(1, NX):
        greet(at_x(mod(m + k, NX)))
    for k in range(1, NY):
        greet(at_yz(mod(y + k, NY), z))
    for k in range(1, NZ):
        greet(at_yz(y, mod(z + k, NZ)))
    greet(sibling)

    def out_peer(k):
        zz = mod(z + k, NZ)
        return at_yz(mod(y + m + zz, NY), zz)

    def in_peer(k):
        return at_yz(mod(y - m - z, NY), mod(z + k, NZ))

    for k in range(1, NZ):
        greet(out_peer(k))
        greet(in_peer(k))

    @pl.when(other_pair)
    def _():
        greet(out_peer(0))
        greet(in_peer(0))

    fixed = NX - 1 + NY - 1 + NZ - 1 + 1 + 2 * (NZ - 1)
    pl.semaphore_wait(barrier, fixed + 2 * other_pair.astype(jnp.int32))

    sent = []

    p1 = []
    for k in range(1, NX):
        copy = rcopy(grad, xg.at[m], p1_s.at[k], p1_r.at[k], at_x(mod(m + k, NX)))
        copy.start()
        sent.append(copy)
    pltpu.make_async_copy(dwg, wg.at[0, z], ld_sem.at[11]).wait()
    for k in range(1, NZ):
        copy = rcopy(wg.at[dp, z], wg.at[dp, z], wz_s.at[k], wz_r.at[k], at_yz(y, mod(z + k, NZ)))
        copy.start()
        sent.append(copy)

    loads[1].wait()
    loads[2].wait()
    col = lax.broadcasted_iota(jnp.int32, (G, RB), 1)
    zc = lax.shift_right_logical(col, 1)
    named = jnp.bitwise_and(y + m + zc, NY - 1) * NZ + zc
    r0 = rt[:, 0:1]
    r1 = rt[:, 1:2]
    hit0 = (r0 == named).astype(F32)
    hit1 = (r1 == named).astype(F32)
    hits = hit0 + hit1
    below = (
        lax.broadcasted_iota(jnp.int32, (G, G), 0) > lax.broadcasted_iota(jnp.int32, (G, G), 1)
    ).astype(BF)
    rank = dot(below, hits.astype(BF), NN)
    taken = (rank == jnp.bitwise_and(col, 1).astype(F32)).astype(F32)
    select = (hits * taken).astype(BF)
    pv = pr[...].astype(F32)
    weights = ((hit0 * pv[:, 0:1] + hit1 * pv[:, 1:2]) * taken).astype(BF)

    loads[0].wait()
    for k in range(1, NX):
        rcopy(grad, xg.at[mod(m - k, NX)], p1_s.at[k], p1_r.at[k], at_x(mod(m - k, NX))).wait_recv()
    for j in range(NX):
        xf[j * T:(j + 1) * T, :] = xg[j].astype(F32)
    xb[...] = xf[...].astype(BF)

    rf[...] = dot(select, xb[...], TN)
    for j in range(NZ):
        s2[j] = rf[2 * j:2 * j + 2, :].astype(BF)

    def exchange(src, dst, ssem, rsem, peer):
        local = pltpu.make_async_copy(src.at[z], dst.at[z], rsem.at[0])

        @pl.when(own_pair)
        def _():
            local.start()

        first = rcopy(src.at[z], dst.at[z], ssem.at[0], rsem.at[0], peer(0))

        @pl.when(other_pair)
        def _():
            first.start()

        for k in range(1, NZ):
            copy = rcopy(src.at[mod(z + k, NZ)], dst.at[z], ssem.at[k], rsem.at[k], peer(k))
            copy.start()
            sent.append(copy)
        return first

    def arrive(src, dst, ssem, rsem, peer):
        for k in range(NZ):
            rcopy(src.at[0], dst.at[mod(z - k, NZ)], ssem.at[k], rsem.at[k], peer(k)).wait_recv()

    p2_first = exchange(s2, r2, p2_s, p2_r, out_peer)

    loads[3].wait()
    loads[4].wait()
    loads[5].wait()
    dense_up = dot(xb[...], dwd_v[...], NT)
    dense_gg, dense_gu = swiglu_back(dense_up, dgp_v[...], dup_v[...])
    gg[y, 0] = dense_gg
    gg[y, 1] = dense_gu

    arrive(s2, r2, p2_s, p2_r, out_peer)
    for j in range(NZ):
        rf[2 * j:2 * j + 2, :] = r2[j].astype(F32)

    def block_of(member):
        return mod(y - z - member, NY)

    mine = block_of(m)
    ag[mine] = rf[...].astype(BF)

    right = at_x(mod(m + 1, NX))
    left = at_x(mod(m - 1, NX))
    far = NX // 2
    near = NX - 1 - far
    hops = [(far, near) if c % 2 == 0 else (near, far) for c in range(C)]

    def cols(c):
        return pl.ds(c * CW, CW)

    def ag_copy(d, t, c):
        step = t if d == 0 else -t
        ref = ag.at[block_of(m - step), :, cols(c)]
        return rcopy(ref, ref, ag_s.at[d, t, c], ag_r.at[d, t, c], (right, left)[d])

    def ag_arrival(d, t, c):
        step = t + 1 if d == 0 else -(t + 1)
        ref = ag.at[block_of(m - step), :, cols(c)]
        rcopy(ref, ref, ag_s.at[d, t, c], ag_r.at[d, t, c], (right, left)[d]).wait_recv()

    for c in range(C):
        for d in range(2):
            if hops[c][d] > 0:
                copy = ag_copy(d, 0, c)
                copy.start()
                sent.append(copy)

    for k in range(1, NY):
        copy = rcopy(gg.at[y], gg.at[y], gg_s.at[k], gg_r.at[k], at_yz(mod(y + k, NY), z))
        copy.start()
        sent.append(copy)
    for k in range(1, NZ):
        rcopy(
            wg.at[dp, z], wg.at[dp, mod(z - k, NZ)], wz_s.at[k], wz_r.at[k], at_yz(y, mod(z + k, NZ))
        ).wait_recv()
    to_sibling = rcopy(wg.at[dp], wg.at[dp], sib.at[0], sib.at[1], sibling)
    to_sibling.start()
    sent.append(to_sibling)

    loads[6].wait()
    for t in range(1, far):
        for c in range(C):
            for d in range(2):
                if t < hops[c][d]:
                    ag_arrival(d, t - 1, c)
                    copy = ag_copy(d, t, c)
                    copy.start()
                    sent.append(copy)
    upstream = jnp.zeros((SL, F), F32)
    for c in range(C):
        for d in range(2):
            if hops[c][d] > 0:
                ag_arrival(d, hops[c][d] - 1, c)
        rows = ag[:, :, c * CW:(c + 1) * CW].reshape(SL, CW)
        upstream = upstream + dot(rows, ewd_v[:, c * CW:(c + 1) * CW], NT)
    loads[7].wait()
    loads[8].wait()
    expert_gg, expert_gu = swiglu_back(upstream, egp_v[...], eup_v[...])

    def rs_copy(d, t, c):
        goal = m + hops[c][0] - t if d == 0 else m - hops[c][1] + t
        src = bk.at[block_of(goal), :, cols(c)] if t == 0 else rs.at[d, t, :, cols(c)]
        return rcopy(src, rr.at[d, t, :, cols(c)], rs_s.at[d, t, c], rs_r.at[d, t, c], (right, left)[d])

    def rs_arrival(d, t, c):
        rcopy(
            bk.at[0, :, cols(c)], rr.at[d, t, :, cols(c)], rs_s.at[d, t, c], rs_r.at[d, t, c], (right, left)[d]
        ).wait_recv()

    loads[9].wait()
    loads[10].wait()
    for c in range(C):
        span = slice(c * CW, (c + 1) * CW)
        back = dot(expert_gg, ewg_v[span, :], NT) + dot(expert_gu, ewu_v[span, :], NT)
        bk[:, :, span] = back.astype(BF).reshape(NY, RB, CW)
        for d in range(2):
            if hops[c][d] > 0:
                copy = rs_copy(d, 0, c)
                copy.start()
                sent.append(copy)

    for k in range(1, NY):
        rcopy(
            gg.at[y], gg.at[mod(y - k, NY)], gg_s.at[k], gg_r.at[k], at_yz(mod(y + k, NY), z)
        ).wait_recv()
    rcopy(wg.at[1 - dp], wg.at[1 - dp], sib.at[0], sib.at[1], sibling).wait_recv()
    dense = jnp.zeros((NY * G, DB), F32)
    for which in range(2):
        for j in range(NZ):
            wf[which, j * DR:(j + 1) * DR, :] = wg[which, j].astype(F32)
        dense = dense + dot(gg[:, which].reshape(NY * G, F), wf[which].astype(BF), NT)
    do_s[...] = dense.astype(BF).reshape(NY, G, DB)
    for k in range(1, NY):
        goal = mod(y + k, NY)
        copy = rcopy(do_s.at[goal], do_r.at[y], do_ss.at[k], do_rs.at[k], at_yz(goal, z))
        copy.start()
        sent.append(copy)
    do_r[y] = do_s[y]

    for t in range(1, far):
        for c in range(C):
            span = slice(c * CW, (c + 1) * CW)
            for d in range(2):
                if t < hops[c][d]:
                    rs_arrival(d, t - 1, c)
                    goal = m + hops[c][0] - t if d == 0 else m - hops[c][1] + t
                    part = rr[d, t - 1, :, span].astype(F32) + bk[block_of(goal), :, span].astype(F32)
                    rs[d, t, :, span] = part.astype(BF)
                    copy = rs_copy(d, t, c)
                    copy.start()
                    sent.append(copy)
    for c in range(C):
        span = slice(c * CW, (c + 1) * CW)
        part = bk[mine, :, span].astype(F32)
        for d in range(2):
            if hops[c][d] > 0:
                rs_arrival(d, hops[c][d] - 1, c)
                part = part + rr[d, hops[c][d] - 1, :, span].astype(F32)
        rf[:, span] = part
    for j in range(NZ):
        s6[j] = rf[2 * j:2 * j + 2, :].astype(BF)

    p6_first = exchange(s6, r6, p6_s, p6_r, in_peer)

    for k in range(1, NY):
        rcopy(
            do_s.at[y], do_r.at[mod(y - k, NY)], do_ss.at[k], do_rs.at[k], at_yz(mod(y + k, NY), z)
        ).wait_recv()
    pair = 2 if (2 * DB) % 128 == 0 and NY % 2 == 0 else NY
    for j in range(0, NY, pair):
        tot[:, j * DB:(j + pair) * DB] = jnp.concatenate(
            [do_r[j + i].astype(F32) for i in range(pair)], axis=1
        )

    arrive(s6, r6, p6_s, p6_r, in_peer)
    for j in range(NZ):
        rf[2 * j:2 * j + 2, :] = r6[j].astype(F32)
    tot[...] = tot[...] + dot(weights, rf[...].astype(BF), NN)

    for j in range(NX):
        s8[j] = tot[j * T:(j + 1) * T, :].astype(BF)
    for k in range(1, NX):
        goal = mod(m + k, NX)
        copy = rcopy(s8.at[goal], r8.at[m], p8_s.at[k], p8_r.at[k], at_x(goal))
        copy.start()
        sent.append(copy)
    total = xg[m].astype(F32) + s8[m].astype(F32)
    for k in range(1, NX):
        source = mod(m - k, NX)
        rcopy(s8.at[0], r8.at[source], p8_s.at[k], p8_r.at[k], at_x(source)).wait_recv()
        total = total + r8[source].astype(F32)
    out[...] = total.astype(BF)

    for copy in sent:
        copy.wait_send()

    @pl.when(other_pair)
    def _():
        p2_first.wait_send()
        p6_first.wait_send()


def body(NX, NY, NZ, *args):
    grad, routes, probs, dgp, dup, dwg, dwu, dwd, egp, eup, ewg, ewu, ewd = args
    T, D = grad.shape
    G = NX * T
    F = dwd.shape[0]
    SL = egp.shape[1]
    RB = SL // NY
    DR = dwg.shape[0]
    DB = DR * NZ
    C = 4
    far = NX // 2
    V = pltpu.VMEM
    dma = pltpu.SemaphoreType.DMA
    scratch = [
        V((NX, T, D), BF), V((G, D), F32), V((G, D), BF), V((G, 2), jnp.int32), V((G, 2), BF),
        V((G, F), BF), V((G, F), BF), V((F, D), BF), V((SL, F), BF), V((SL, F), BF),
        V((F, D), BF), V((D, F), BF), V((D, F), BF),
        V((2, NZ, DR, F), BF), V((2, DB, F), F32), V((NY, 2, G, F), BF),
        V((NY, G, DB), BF), V((NY, G, DB), BF), V((RB, D), F32),
        V((NZ, 2, D), BF), V((NZ, 2, D), BF), V((NZ, 2, D), BF), V((NZ, 2, D), BF),
        V((NY, RB, D), BF), V((NY, RB, D), BF),
        V((2, far, RB, D), BF), V((2, far, RB, D), BF),
        V((NX, T, D), BF), V((NX, T, D), BF), V((G, D), F32),
        dma((12,)), dma((NX,)), dma((NX,)), dma((NZ,)), dma((NZ,)), dma((2,)),
        dma((NY,)), dma((NY,)), dma((NY,)), dma((NY,)),
        dma((NZ,)), dma((NZ,)), dma((NZ,)), dma((NZ,)),
        dma((2, far, C)), dma((2, far, C)), dma((2, far, C)), dma((2, far, C)),
        dma((NX,)), dma((NX,)),
    ]
    flops = 2 * 3 * F * D * (SL + G)
    return pl.pallas_call(
        functools.partial(kernel, NX, NY, NZ, C),
        out_shape=jax.ShapeDtypeStruct((T, D), BF),
        in_specs=[pl.BlockSpec(memory_space=pl.ANY)] * 13,
        out_specs=pl.BlockSpec(memory_space=pltpu.VMEM),
        scratch_shapes=scratch,
        compiler_params=pltpu.CompilerParams(
            collective_id=0, has_side_effects=True, vmem_limit_bytes=48 * 1024 * 1024
        ),
        cost_estimate=pl.CostEstimate(
            flops=flops, bytes_accessed=8 * F * D, transcendentals=F * (SL + G)
        ),
        name="layer_back",
    )(*args)


def solution(mesh):
    NX = mesh.shape["tensor"]
    NE = mesh.shape["expert"]
    NY = NX
    NZ = NE // NY
    return jax.shard_map(
        functools.partial(body, NX, NY, NZ),
        mesh=mesh,
        in_specs=(
            P(("dp", "expert", "tensor"), None),
            P(("dp", "expert"), None),
            P(("dp", "expert"), None),
            P(("dp", "expert"), "tensor"),
            P(("dp", "expert"), "tensor"),
            P("expert", "tensor"),
            P("expert", "tensor"),
            P("tensor", None),
            P(("dp", "expert"), None, "tensor"),
            P(("dp", "expert"), None, "tensor"),
            P("expert", None, "tensor"),
            P("expert", None, "tensor"),
            P("expert", "tensor", None),
        ),
        out_specs=P(("dp", "expert", "tensor"), None),
        check_vma=False,
    )
```

```python
import functools
import math

import jax
import jax.numpy as jnp
from jax import lax
from jax.experimental import pallas as pl
from jax.experimental.pallas import tpu as pltpu
from jax.sharding import PartitionSpec as P

BF = jnp.bfloat16
F32 = jnp.float32
NT = (((1,), (1,)), ((), ()))
TN = (((0,), (0,)), ((), ()))
NN = (((1,), (0,)), ((), ()))


def mod(value, n):
    return lax.rem(value + 4 * n, n)


def dot(a, b, dims):
    return lax.dot_general(a, b, dims, preferred_element_type=F32)


def swiglu_back(upstream, gate_pre, up_pre):
    gate = gate_pre.astype(F32)
    up = up_pre.astype(F32)
    sigma = 1.0 / (1.0 + jnp.exp(-gate))
    grad_gate = upstream * up * (sigma * (1.0 + gate * (1.0 - sigma)))
    grad_up = upstream * (gate * sigma)
    return grad_gate, grad_up


def kernel(
    NX, NY, NZ, C,
    grad, routes, probs, dgp, dup, dwg, dwu, dwd, egp, eup, ewg, ewu, ewd,
    out,
    xg, xf, xb, rt, pr, dgp_v, dup_v, dwd_v, egp_v, eup_v, ewd_v, ewg_v, ewu_v,
    wg, wf, gg, do_s, do_r, rf, s2, r2, s6, r6, ag, bk, rr, rs, s8, r8, tot,
    ld_sem, p1_s, p1_r, wz_s, wz_r, sib, gg_s, gg_r, do_ss, do_rs,
    p2_s, p2_r, p6_s, p6_r, ag_s, ag_r, rs_s, rs_r, p8_s, p8_r,
):
    T, D = grad.shape
    G = NX * T
    F = dwd.shape[0]
    RB = ag.shape[1]
    CW = D // C
    DB = do_s.shape[2]
    DR = dwg.shape[0]
    SL = NY * RB

    dp = lax.axis_index("dp")
    ex = lax.axis_index("expert")
    m = lax.axis_index("tensor")
    y = ex // NZ
    z = ex % NZ

    def rcopy(src, dst, ss, rsem, device):
        return pltpu.make_async_remote_copy(
            src_ref=src, dst_ref=dst, send_sem=ss, recv_sem=rsem,
            device_id=device, device_id_type=pl.DeviceIdType.MESH,
        )

    def at_x(x):
        return (dp, ex, x)

    def at_yz(yy, zz):
        return (dp, yy * NZ + zz, m)

    sibling = (1 - dp, ex, m)
    own_pair = mod(m + z, NY) == 0
    other_pair = jnp.logical_not(own_pair)

    loads = [
        pltpu.make_async_copy(grad, xg.at[m], ld_sem.at[0]),
        pltpu.make_async_copy(routes, rt, ld_sem.at[1]),
        pltpu.make_async_copy(probs, pr, ld_sem.at[2]),
        pltpu.make_async_copy(dwd, dwd_v, ld_sem.at[3]),
        pltpu.make_async_copy(dgp, dgp_v, ld_sem.at[4]),
        pltpu.make_async_copy(dup, dup_v, ld_sem.at[5]),
        pltpu.make_async_copy(ewd.at[0], ewd_v, ld_sem.at[6]),
        pltpu.make_async_copy(egp.at[0], egp_v, ld_sem.at[7]),
        pltpu.make_async_copy(eup.at[0], eup_v, ld_sem.at[8]),
        pltpu.make_async_copy(ewg.at[0], ewg_v, ld_sem.at[9]),
        pltpu.make_async_copy(ewu.at[0], ewu_v, ld_sem.at[10]),
    ]
    own_gate = pltpu.make_async_copy(dwg, wg.at[0, z], ld_sem.at[11])
    own_up = pltpu.make_async_copy(dwu, wg.at[1, z], ld_sem.at[11])

    @pl.when(dp == 0)
    def _():
        own_gate.start()

    @pl.when(dp == 1)
    def _():
        own_up.start()

    for load in loads:
        load.start()

    barrier = pltpu.get_barrier_semaphore()

    def greet(device):
        pl.semaphore_signal(barrier, inc=1, device_id=device, device_id_type=pl.DeviceIdType.MESH)

    for k in range(1, NX):
        greet(at_x(mod(m + k, NX)))
    for k in range(1, NY):
        greet(at_yz(mod(y + k, NY), z))
    for k in range(1, NZ):
        greet(at_yz(y, mod(z + k, NZ)))
    greet(sibling)

    def out_peer(k):
        zz = mod(z + k, NZ)
        return at_yz(mod(y + m + zz, NY), zz)

    def in_peer(k):
        return at_yz(mod(y - m - z, NY), mod(z + k, NZ))

    for k in range(1, NZ):
        greet(out_peer(k))
        greet(in_peer(k))

    @pl.when(other_pair)
    def _():
        greet(out_peer(0))
        greet(in_peer(0))

    fixed = NX - 1 + NY - 1 + NZ - 1 + 1 + 2 * (NZ - 1)
    pl.semaphore_wait(barrier, fixed + 2 * other_pair.astype(jnp.int32))

    sent = []

    p1 = []
    for k in range(1, NX):
        copy = rcopy(grad, xg.at[m], p1_s.at[k], p1_r.at[k], at_x(mod(m + k, NX)))
        copy.start()
        sent.append(copy)
    pltpu.make_async_copy(dwg, wg.at[0, z], ld_sem.at[11]).wait()
    for k in range(1, NZ):
        copy = rcopy(wg.at[dp, z], wg.at[dp, z], wz_s.at[k], wz_r.at[k], at_yz(y, mod(z + k, NZ)))
        copy.start()
        sent.append(copy)

    loads[1].wait()
    loads[2].wait()
    slot = lax.broadcasted_iota(jnp.int32, (RB, G), 0)
    zc = lax.shift_right_logical(slot, 1)
    named = jnp.bitwise_and(y + m + zc, NY - 1) * NZ + zc
    r0 = rt[0:1, :]
    r1 = rt[1:2, :]
    hit0 = (r0 == named).astype(F32)
    hit1 = (r1 == named).astype(F32)
    hits = hit0 + hit1
    earlier = (
        lax.broadcasted_iota(jnp.int32, (G, G), 0) < lax.broadcasted_iota(jnp.int32, (G, G), 1)
    ).astype(BF)
    rank = dot(hits.astype(BF), earlier, NN)
    taken = (rank == jnp.bitwise_and(slot, 1).astype(F32)).astype(F32)
    select = (hits * taken).astype(BF)
    pv = pr[...].astype(F32)
    weights = ((hit0 * pv[0:1, :] + hit1 * pv[1:2, :]) * taken).astype(BF)

    loads[0].wait()
    for k in range(1, NX):
        rcopy(grad, xg.at[mod(m - k, NX)], p1_s.at[k], p1_r.at[k], at_x(mod(m - k, NX))).wait_recv()
    for j in range(NX):
        xf[j * T:(j + 1) * T, :] = xg[j].astype(F32)
    xb[...] = xf[...].astype(BF)

    rf[...] = dot(select, xb[...], NN)
    for j in range(NZ):
        s2[j] = rf[2 * j:2 * j + 2, :].astype(BF)

    def exchange(src, dst, ssem, rsem, peer):
        local = pltpu.make_async_copy(src.at[z], dst.at[z], rsem.at[0])

        @pl.when(own_pair)
        def _():
            local.start()

        first = rcopy(src.at[z], dst.at[z], ssem.at[0], rsem.at[0], peer(0))

        @pl.when(other_pair)
        def _():
            first.start()

        for k in range(1, NZ):
            copy = rcopy(src.at[mod(z + k, NZ)], dst.at[z], ssem.at[k], rsem.at[k], peer(k))
            copy.start()
            sent.append(copy)
        return first

    def arrive(src, dst, ssem, rsem, peer):
        for k in range(NZ):
            rcopy(src.at[0], dst.at[mod(z - k, NZ)], ssem.at[k], rsem.at[k], peer(k)).wait_recv()

    p2_first = exchange(s2, r2, p2_s, p2_r, out_peer)

    loads[3].wait()
    loads[4].wait()
    loads[5].wait()
    dense_up = dot(xb[...], dwd_v[...], NT)
    dense_gg, dense_gu = swiglu_back(dense_up, dgp_v[...], dup_v[...])
    gg[y, 0] = dense_gg.astype(BF)
    gg[y, 1] = dense_gu.astype(BF)

    arrive(s2, r2, p2_s, p2_r, out_peer)
    for j in range(NZ):
        rf[2 * j:2 * j + 2, :] = r2[j].astype(F32)

    def block_of(member):
        return mod(y - z - member, NY)

    mine = block_of(m)
    ag[mine] = rf[...].astype(BF)

    right = at_x(mod(m + 1, NX))
    left = at_x(mod(m - 1, NX))
    far = NX // 2
    near = NX - 1 - far
    hops = [(far, near) if c % 2 == 0 else (near, far) for c in range(C)]

    def cols(c):
        return pl.ds(c * CW, CW)

    def ag_copy(d, t, c):
        step = t if d == 0 else -t
        ref = ag.at[block_of(m - step), :, cols(c)]
        return rcopy(ref, ref, ag_s.at[d, t, c], ag_r.at[d, t, c], (right, left)[d])

    def ag_arrival(d, t, c):
        step = t + 1 if d == 0 else -(t + 1)
        ref = ag.at[block_of(m - step), :, cols(c)]
        rcopy(ref, ref, ag_s.at[d, t, c], ag_r.at[d, t, c], (right, left)[d]).wait_recv()

    for c in range(C):
        for d in range(2):
            if hops[c][d] > 0:
                copy = ag_copy(d, 0, c)
                copy.start()
                sent.append(copy)

    for k in range(1, NY):
        copy = rcopy(gg.at[y], gg.at[y], gg_s.at[k], gg_r.at[k], at_yz(mod(y + k, NY), z))
        copy.start()
        sent.append(copy)
    for k in range(1, NZ):
        rcopy(
            wg.at[dp, z], wg.at[dp, mod(z - k, NZ)], wz_s.at[k], wz_r.at[k], at_yz(y, mod(z + k, NZ))
        ).wait_recv()
    to_sibling = rcopy(wg.at[dp], wg.at[dp], sib.at[0], sib.at[1], sibling)
    to_sibling.start()
    sent.append(to_sibling)

    loads[6].wait()
    for t in range(1, far):
        for c in range(C):
            for d in range(2):
                if t < hops[c][d]:
                    ag_arrival(d, t - 1, c)
                    copy = ag_copy(d, t, c)
                    copy.start()
                    sent.append(copy)
    upstream = jnp.zeros((F, SL), F32)
    for c in range(C):
        for d in range(2):
            if hops[c][d] > 0:
                ag_arrival(d, hops[c][d] - 1, c)
        rows = ag[:, :, c * CW:(c + 1) * CW].reshape(SL, CW)
        upstream = upstream + dot(ewd_v[:, c * CW:(c + 1) * CW], rows, NT)
    loads[7].wait()
    loads[8].wait()
    expert_gg, expert_gu = [
        jnp.transpose(part).astype(BF) for part in swiglu_back(upstream, egp_v[...], eup_v[...])
    ]

    def rs_copy(d, t, c):
        goal = m + hops[c][0] - t if d == 0 else m - hops[c][1] + t
        src = bk.at[block_of(goal), :, cols(c)] if t == 0 else rs.at[d, t, :, cols(c)]
        return rcopy(src, rr.at[d, t, :, cols(c)], rs_s.at[d, t, c], rs_r.at[d, t, c], (right, left)[d])

    def rs_arrival(d, t, c):
        rcopy(
            bk.at[0, :, cols(c)], rr.at[d, t, :, cols(c)], rs_s.at[d, t, c], rs_r.at[d, t, c], (right, left)[d]
        ).wait_recv()

    loads[9].wait()
    loads[10].wait()
    for c in range(C):
        span = slice(c * CW, (c + 1) * CW)
        back = dot(expert_gg, ewg_v[:, span], NN) + dot(expert_gu, ewu_v[:, span], NN)
        bk[:, :, span] = back.astype(BF).reshape(NY, RB, CW)
        for d in range(2):
            if hops[c][d] > 0:
                copy = rs_copy(d, 0, c)
                copy.start()
                sent.append(copy)

    for k in range(1, NY):
        rcopy(
            gg.at[y], gg.at[mod(y - k, NY)], gg_s.at[k], gg_r.at[k], at_yz(mod(y + k, NY), z)
        ).wait_recv()
    rcopy(wg.at[1 - dp], wg.at[1 - dp], sib.at[0], sib.at[1], sibling).wait_recv()
    dense = jnp.zeros((NY * G, DB), F32)
    for which in range(2):
        for j in range(NZ):
            wf[which, j * DR:(j + 1) * DR, :] = wg[which, j].astype(F32)
        dense = dense + dot(gg[:, which].reshape(NY * G, F), wf[which].astype(BF), NT)
    do_s[...] = dense.astype(BF).reshape(NY, G, DB)
    for k in range(1, NY):
        goal = mod(y + k, NY)
        copy = rcopy(do_s.at[goal], do_r.at[y], do_ss.at[k], do_rs.at[k], at_yz(goal, z))
        copy.start()
        sent.append(copy)
    do_r[y] = do_s[y]

    for t in range(1, far):
        for c in range(C):
            span = slice(c * CW, (c + 1) * CW)
            for d in range(2):
                if t < hops[c][d]:
                    rs_arrival(d, t - 1, c)
                    goal = m + hops[c][0] - t if d == 0 else m - hops[c][1] + t
                    part = rr[d, t - 1, :, span].astype(F32) + bk[block_of(goal), :, span].astype(F32)
                    rs[d, t, :, span] = part.astype(BF)
                    copy = rs_copy(d, t, c)
                    copy.start()
                    sent.append(copy)
    for c in range(C):
        span = slice(c * CW, (c + 1) * CW)
        part = bk[mine, :, span].astype(F32)
        for d in range(2):
            if hops[c][d] > 0:
                rs_arrival(d, hops[c][d] - 1, c)
                part = part + rr[d, hops[c][d] - 1, :, span].astype(F32)
        rf[:, span] = part
    for j in range(NZ):
        s6[j] = rf[2 * j:2 * j + 2, :].astype(BF)

    p6_first = exchange(s6, r6, p6_s, p6_r, in_peer)

    for k in range(1, NY):
        rcopy(
            do_s.at[y], do_r.at[mod(y - k, NY)], do_ss.at[k], do_rs.at[k], at_yz(mod(y + k, NY), z)
        ).wait_recv()
    pair = 2 if (2 * DB) % 128 == 0 and NY % 2 == 0 else NY
    for j in range(0, NY, pair):
        tot[:, j * DB:(j + pair) * DB] = jnp.concatenate(
            [do_r[j + i].astype(F32) for i in range(pair)], axis=1
        )

    arrive(s6, r6, p6_s, p6_r, in_peer)
    for j in range(NZ):
        rf[2 * j:2 * j + 2, :] = r6[j].astype(F32)
    tot[...] = tot[...] + dot(weights, rf[...].astype(BF), TN)

    for j in range(NX):
        s8[j] = tot[j * T:(j + 1) * T, :].astype(BF)
    for k in range(1, NX):
        goal = mod(m + k, NX)
        copy = rcopy(s8.at[goal], r8.at[m], p8_s.at[k], p8_r.at[k], at_x(goal))
        copy.start()
        sent.append(copy)
    total = xg[m].astype(F32) + s8[m].astype(F32)
    for k in range(1, NX):
        source = mod(m - k, NX)
        rcopy(s8.at[0], r8.at[source], p8_s.at[k], p8_r.at[k], at_x(source)).wait_recv()
        total = total + r8[source].astype(F32)
    out[...] = total.astype(BF)

    for copy in sent:
        copy.wait_send()

    @pl.when(other_pair)
    def _():
        p2_first.wait_send()
        p6_first.wait_send()


def body(NX, NY, NZ, *args):
    grad, routes, probs, dgp, dup, dwg, dwu, dwd, egp, eup, ewg, ewu, ewd = args
    T, D = grad.shape
    G = NX * T
    F = dwd.shape[0]
    SL = egp.shape[1]
    routes, probs = routes.T, probs.T
    egp, eup, ewg, ewu = [jnp.swapaxes(part, 1, 2) for part in (egp, eup, ewg, ewu)]
    RB = SL // NY
    DR = dwg.shape[0]
    DB = DR * NZ
    C = 4
    far = NX // 2
    V = pltpu.VMEM
    dma = pltpu.SemaphoreType.DMA
    scratch = [
        V((NX, T, D), BF), V((G, D), F32), V((G, D), BF), V((2, G), jnp.int32), V((2, G), BF),
        V((G, F), BF), V((G, F), BF), V((F, D), BF), V((F, SL), BF), V((F, SL), BF),
        V((F, D), BF), V((F, D), BF), V((F, D), BF),
        V((2, NZ, DR, F), BF), V((2, DB, F), F32), V((NY, 2, G, F), BF),
        V((NY, G, DB), BF), V((NY, G, DB), BF), V((RB, D), F32),
        V((NZ, 2, D), BF), V((NZ, 2, D), BF), V((NZ, 2, D), BF), V((NZ, 2, D), BF),
        V((NY, RB, D), BF), V((NY, RB, D), BF),
        V((2, far, RB, D), BF), V((2, far, RB, D), BF),
        V((NX, T, D), BF), V((NX, T, D), BF), V((G, D), F32),
        dma((12,)), dma((NX,)), dma((NX,)), dma((NZ,)), dma((NZ,)), dma((2,)),
        dma((NY,)), dma((NY,)), dma((NY,)), dma((NY,)),
        dma((NZ,)), dma((NZ,)), dma((NZ,)), dma((NZ,)),
        dma((2, far, C)), dma((2, far, C)), dma((2, far, C)), dma((2, far, C)),
        dma((NX,)), dma((NX,)),
    ]
    flops = 2 * 3 * F * D * (SL + G)
    return pl.pallas_call(
        functools.partial(kernel, NX, NY, NZ, C),
        out_shape=jax.ShapeDtypeStruct((T, D), BF),
        in_specs=[pl.BlockSpec(memory_space=pl.ANY)] * 13,
        out_specs=pl.BlockSpec(memory_space=pltpu.VMEM),
        scratch_shapes=scratch,
        compiler_params=pltpu.CompilerParams(
            collective_id=0, has_side_effects=True, vmem_limit_bytes=62 * 1024 * 1024
        ),
        cost_estimate=pl.CostEstimate(
            flops=flops, bytes_accessed=8 * F * D, transcendentals=F * (SL + G)
        ),
        name="layer_back",
    )(grad, routes, probs, dgp, dup, dwg, dwu, dwd, egp, eup, ewg, ewu, ewd)


def solution(mesh):
    NX = mesh.shape["tensor"]
    NE = mesh.shape["expert"]
    NY = NX
    NZ = NE // NY
    return jax.shard_map(
        functools.partial(body, NX, NY, NZ),
        mesh=mesh,
        in_specs=(
            P(("dp", "expert", "tensor"), None),
            P(("dp", "expert"), None),
            P(("dp", "expert"), None),
            P(("dp", "expert"), "tensor"),
            P(("dp", "expert"), "tensor"),
            P("expert", "tensor"),
            P("expert", "tensor"),
            P("tensor", None),
            P(("dp", "expert"), None, "tensor"),
            P(("dp", "expert"), None, "tensor"),
            P("expert", None, "tensor"),
            P("expert", None, "tensor"),
            P("expert", "tensor", None),
        ),
        out_specs=P(("dp", "expert", "tensor"), None),
        check_vma=False,
    )
```

```python
import functools
import math

import jax
import jax.numpy as jnp
from jax import lax
from jax.experimental import pallas as pl
from jax.experimental.pallas import tpu as pltpu
from jax.sharding import PartitionSpec as P

BF = jnp.bfloat16
F32 = jnp.float32
NT = (((1,), (1,)), ((), ()))
TN = (((0,), (0,)), ((), ()))
NN = (((1,), (0,)), ((), ()))


def mod(value, n):
    return lax.rem(value + 4 * n, n)


def dot(a, b, dims):
    return lax.dot_general(a, b, dims, preferred_element_type=F32)


def swiglu_back(upstream, gate_pre, up_pre):
    gate = gate_pre.astype(F32)
    up = up_pre.astype(F32)
    sigma = 1.0 / (1.0 + jnp.exp(-gate))
    grad_gate = upstream * up * (sigma * (1.0 + gate * (1.0 - sigma)))
    grad_up = upstream * (gate * sigma)
    return grad_gate, grad_up


def kernel(
    NX, NY, NZ, C,
    grad, routes, probs, dgp, dup, dwg, dwu, dwd, egp, eup, ewg, ewu, ewd,
    out,
    xg, xf, xb, rt, pr, dgp_v, dup_v, dwd_v, egp_v, eup_v, ewd_v, ewg_v, ewu_v,
    wg, wf, gg, do_s, do_r, rf, rg, s2, r2, s6, r6, ag, bk, rr, rs, s8, r8, tot,
    ld_sem, p1_s, p1_r, wz_s, wz_r, sib, gg_s, gg_r, do_ss, do_rs,
    p2_s, p2_r, p6_s, p6_r, ag_s, ag_r, rs_s, rs_r, p8_s, p8_r,
):
    T, D = grad.shape
    G = NX * T
    F = dwd.shape[0]
    RB = ag.shape[1]
    CW = D // C
    DB = do_s.shape[2]
    DR = dwg.shape[0]
    SL = NY * RB

    dp = lax.axis_index("dp")
    ex = lax.axis_index("expert")
    m = lax.axis_index("tensor")
    y = ex // NZ
    z = ex % NZ

    def rcopy(src, dst, ss, rsem, device):
        return pltpu.make_async_remote_copy(
            src_ref=src, dst_ref=dst, send_sem=ss, recv_sem=rsem,
            device_id=device, device_id_type=pl.DeviceIdType.MESH,
        )

    def at_x(x):
        return (dp, ex, x)

    def at_yz(yy, zz):
        return (dp, yy * NZ + zz, m)

    sibling = (1 - dp, ex, m)
    own_pair = mod(m + z, NY) == 0
    other_pair = jnp.logical_not(own_pair)

    barrier = pltpu.get_barrier_semaphore()

    def greet(device):
        pl.semaphore_signal(barrier, inc=1, device_id=device, device_id_type=pl.DeviceIdType.MESH)

    def out_peer(k):
        zz = mod(z + k, NZ)
        return at_yz(mod(y + m + zz, NY), zz)

    def in_peer(k):
        return at_yz(mod(y - m - z, NY), mod(z + k, NZ))

    for k in range(1, NX):
        greet(at_x(mod(m + k, NX)))
    for k in range(1, NZ):
        greet(in_peer(k))
        greet(out_peer(k))

    @pl.when(other_pair)
    def _():
        greet(in_peer(0))
        greet(out_peer(0))

    for k in range(1, NZ):
        greet(at_yz(y, mod(z + k, NZ)))
    for k in range(1, NY):
        greet(at_yz(mod(y + k, NY), z))
    greet(sibling)

    loads = [
        pltpu.make_async_copy(grad, xg.at[m], ld_sem.at[0]),
        pltpu.make_async_copy(routes, rt, ld_sem.at[1]),
        pltpu.make_async_copy(probs, pr, ld_sem.at[2]),
        pltpu.make_async_copy(dwd, dwd_v, ld_sem.at[3]),
        pltpu.make_async_copy(dgp, dgp_v, ld_sem.at[4]),
        pltpu.make_async_copy(dup, dup_v, ld_sem.at[5]),
        pltpu.make_async_copy(ewd.at[0], ewd_v, ld_sem.at[6]),
        pltpu.make_async_copy(egp.at[0], egp_v, ld_sem.at[7]),
        pltpu.make_async_copy(eup.at[0], eup_v, ld_sem.at[8]),
        pltpu.make_async_copy(ewg.at[0], ewg_v, ld_sem.at[9]),
        pltpu.make_async_copy(ewu.at[0], ewu_v, ld_sem.at[10]),
    ]
    own_gate = pltpu.make_async_copy(dwg, wg.at[0, z], ld_sem.at[11])
    own_up = pltpu.make_async_copy(dwu, wg.at[1, z], ld_sem.at[11])
    for load in loads[:3]:
        load.start()

    @pl.when(dp == 0)
    def _():
        own_gate.start()

    @pl.when(dp == 1)
    def _():
        own_up.start()

    for load in loads[3:]:
        load.start()

    fixed = NX - 1 + NY - 1 + NZ - 1 + 1 + 2 * (NZ - 1)
    pl.semaphore_wait(barrier, fixed + 2 * other_pair.astype(jnp.int32))

    sent = []

    def send(copy):
        copy.start()
        sent.append(copy)

    def flush():
        for copy in sent:
            copy.wait_send()
        sent.clear()

    H = 2
    HW = D // H

    def half(h):
        return pl.ds(h * HW, HW)

    def span(h):
        return slice(h * HW, (h + 1) * HW)

    order = sorted(range(1, NX), key=lambda k: -min(k, NX - k))

    for h in range(H):
        for k in order:
            send(rcopy(
                grad.at[:, half(h)], xg.at[m, :, half(h)], p1_s.at[h, k], p1_r.at[h, k], at_x(mod(m + k, NX))
            ))

    loads[1].wait()
    loads[2].wait()
    slot = lax.broadcasted_iota(jnp.int32, (RB, G), 0)
    zc = lax.shift_right_logical(slot, 1)
    named = jnp.bitwise_and(y + m + zc, NY - 1) * NZ + zc
    r0 = rt[0:1, :]
    r1 = rt[1:2, :]
    hit0 = (r0 == named).astype(F32)
    hit1 = (r1 == named).astype(F32)
    hits = hit0 + hit1
    earlier = (
        lax.broadcasted_iota(jnp.int32, (G, G), 0) < lax.broadcasted_iota(jnp.int32, (G, G), 1)
    ).astype(BF)
    rank = dot(hits.astype(BF), earlier, NN)
    taken = (rank == jnp.bitwise_and(slot, 1).astype(F32)).astype(F32)
    select = (hits * taken).astype(BF)
    pv = pr[...].astype(F32)
    weights = ((hit0 * pv[0:1, :] + hit1 * pv[1:2, :]) * taken).astype(BF)

    pltpu.make_async_copy(dwg, wg.at[0, z], ld_sem.at[11]).wait()
    for k in range(1, NZ):
        send(rcopy(wg.at[dp, z], wg.at[dp, z], wz_s.at[k], wz_r.at[k], at_yz(y, mod(z + k, NZ))))

    firsts = []

    def exchange(src, dst, ssem, rsem, peer, h):
        local = pltpu.make_async_copy(src.at[z, :, half(h)], dst.at[z, :, half(h)], rsem.at[h, 0])

        @pl.when(own_pair)
        def _():
            local.start()

        first = rcopy(
            src.at[z, :, half(h)], dst.at[z, :, half(h)], ssem.at[h, 0], rsem.at[h, 0], peer(0)
        )

        @pl.when(other_pair)
        def _():
            first.start()

        firsts.append(first)
        for k in range(1, NZ):
            send(rcopy(
                src.at[mod(z + k, NZ), :, half(h)], dst.at[z, :, half(h)], ssem.at[h, k], rsem.at[h, k], peer(k)
            ))

    def arrive(src, dst, ssem, rsem, peer, h):
        for k in range(NZ):
            rcopy(
                src.at[0, :, half(h)], dst.at[mod(z - k, NZ), :, half(h)], ssem.at[h, k], rsem.at[h, k], peer(k)
            ).wait_recv()

    loads[0].wait()
    for h in range(H):
        for k in order:
            source = mod(m - k, NX)
            rcopy(
                grad.at[:, half(h)], xg.at[source, :, half(h)], p1_s.at[h, k], p1_r.at[h, k], at_x(source)
            ).wait_recv()
        for j in range(NX):
            xf[j * T:(j + 1) * T, span(h)] = xg[j, :, span(h)].astype(F32)
        xb[:, span(h)] = xf[:, span(h)].astype(BF)
        rf[:, span(h)] = dot(select, xb[:, span(h)], NN)
        for j in range(NZ):
            s2[j, :, span(h)] = rf[2 * j:2 * j + 2, span(h)].astype(BF)
        exchange(s2, r2, p2_s, p2_r, out_peer, h)

    def block_of(member):
        return mod(y - z - member, NY)

    mine = block_of(m)
    right = at_x(mod(m + 1, NX))
    left = at_x(mod(m - 1, NX))
    far = NX // 2
    near = NX - 1 - far
    hops = [(far, near) if c % 2 == 0 else (near, far) for c in range(C)]
    per = C // H

    def cols(c):
        return pl.ds(c * CW, CW)

    def ag_copy(d, t, c):
        step = t if d == 0 else -t
        ref = ag.at[block_of(m - step), :, cols(c)]
        return rcopy(ref, ref, ag_s.at[d, t, c], ag_r.at[d, t, c], (right, left)[d])

    def ag_arrival(d, t, c):
        step = t + 1 if d == 0 else -(t + 1)
        ref = ag.at[block_of(m - step), :, cols(c)]
        rcopy(ref, ref, ag_s.at[d, t, c], ag_r.at[d, t, c], (right, left)[d]).wait_recv()

    for h in range(H):
        arrive(s2, r2, p2_s, p2_r, out_peer, h)
        for j in range(NZ):
            rg[2 * j:2 * j + 2, span(h)] = r2[j, :, span(h)].astype(F32)
        ag[mine, :, span(h)] = rg[:, span(h)].astype(BF)
        for c in range(h * per, (h + 1) * per):
            for d in range(2):
                if hops[c][d] > 0:
                    send(ag_copy(d, 0, c))

    loads[3].wait()
    loads[4].wait()
    loads[5].wait()
    dense_up = jnp.transpose(dot(dwd_v[...], xb[...], NT))
    dense_gg, dense_gu = swiglu_back(dense_up, dgp_v[...], dup_v[...])
    gg[y, 0] = dense_gg.astype(BF)
    gg[y, 1] = dense_gu.astype(BF)
    for k in range(1, NY):
        send(rcopy(gg.at[y], gg.at[y], gg_s.at[k], gg_r.at[k], at_yz(mod(y + k, NY), z)))

    def pass_on():
        for k in range(1, NZ):
            rcopy(
                wg.at[dp, z], wg.at[dp, mod(z - k, NZ)], wz_s.at[k], wz_r.at[k], at_yz(y, mod(z + k, NZ))
            ).wait_recv()
        send(rcopy(wg.at[dp], wg.at[dp], sib.at[0], sib.at[1], sibling))

    loads[6].wait()
    for t in range(1, far):
        for c in range(C):
            for d in range(2):
                if t < hops[c][d]:
                    ag_arrival(d, t - 1, c)
                    send(ag_copy(d, t, c))
        if t == 1:
            pass_on()
    if far == 1:
        pass_on()
    upstream = jnp.zeros((F, SL), F32)
    for c in range(C):
        for d in range(2):
            if hops[c][d] > 0:
                ag_arrival(d, hops[c][d] - 1, c)
        rows = ag[:, :, c * CW:(c + 1) * CW].reshape(SL, CW)
        upstream = upstream + dot(ewd_v[:, c * CW:(c + 1) * CW], rows, NT)
    loads[7].wait()
    loads[8].wait()
    expert_gg, expert_gu = [
        jnp.transpose(part).astype(BF) for part in swiglu_back(upstream, egp_v[...], eup_v[...])
    ]

    def rs_copy(d, t, c):
        goal = m + hops[c][0] - t if d == 0 else m - hops[c][1] + t
        src = bk.at[block_of(goal), :, cols(c)] if t == 0 else rs.at[d, t, :, cols(c)]
        return rcopy(src, rr.at[d, t, :, cols(c)], rs_s.at[d, t, c], rs_r.at[d, t, c], (right, left)[d])

    def rs_arrival(d, t, c):
        rcopy(
            bk.at[0, :, cols(c)], rr.at[d, t, :, cols(c)], rs_s.at[d, t, c], rs_r.at[d, t, c], (right, left)[d]
        ).wait_recv()

    loads[9].wait()
    loads[10].wait()
    for c in range(C):
        part = slice(c * CW, (c + 1) * CW)
        back = dot(expert_gg, ewg_v[:, part], NN) + dot(expert_gu, ewu_v[:, part], NN)
        bk[:, :, part] = back.astype(BF).reshape(NY, RB, CW)
        for d in range(2):
            if hops[c][d] > 0:
                send(rs_copy(d, 0, c))

    def rs_steps(t):
        for c in range(C):
            part = slice(c * CW, (c + 1) * CW)
            for d in range(2):
                if t < hops[c][d]:
                    rs_arrival(d, t - 1, c)
                    goal = m + hops[c][0] - t if d == 0 else m - hops[c][1] + t
                    both = rr[d, t - 1, :, part].astype(F32) + bk[block_of(goal), :, part].astype(F32)
                    rs[d, t, :, part] = both.astype(BF)
                    send(rs_copy(d, t, c))

    for k in range(1, NY):
        rcopy(
            gg.at[y], gg.at[mod(y - k, NY)], gg_s.at[k], gg_r.at[k], at_yz(mod(y + k, NY), z)
        ).wait_recv()
    rcopy(wg.at[1 - dp], wg.at[1 - dp], sib.at[0], sib.at[1], sibling).wait_recv()
    dense = jnp.zeros((NY * G, DB), F32)
    for which in range(2):
        for j in range(NZ):
            wf[which, j * DR:(j + 1) * DR, :] = wg[which, j].astype(F32)
        dense = dense + dot(gg[:, which].reshape(NY * G, F), wf[which].astype(BF), NT)
    do_s[...] = dense.astype(BF).reshape(NY, G, DB)
    for k in range(1, NY):
        goal = mod(y + k, NY)
        send(rcopy(do_s.at[goal], do_r.at[y], do_ss.at[k], do_rs.at[k], at_yz(goal, z)))
    do_r[y] = do_s[y]

    for t in range(1, far):
        rs_steps(t)
        if t == 1:
            flush()
    for k in range(1, NY):
        rcopy(
            do_s.at[y], do_r.at[mod(y - k, NY)], do_ss.at[k], do_rs.at[k], at_yz(mod(y + k, NY), z)
        ).wait_recv()
    pair = 2 if (2 * DB) % 128 == 0 and NY % 2 == 0 else NY
    for j in range(0, NY, pair):
        tot[:, j * DB:(j + pair) * DB] = jnp.concatenate(
            [do_r[j + i].astype(F32) for i in range(pair)], axis=1
        )

    for h in range(H):
        for c in range(h * per, (h + 1) * per):
            part = slice(c * CW, (c + 1) * CW)
            full = bk[mine, :, part].astype(F32)
            for d in range(2):
                if hops[c][d] > 0:
                    rs_arrival(d, hops[c][d] - 1, c)
                    full = full + rr[d, hops[c][d] - 1, :, part].astype(F32)
            rf[:, part] = full
        for j in range(NZ):
            s6[j, :, span(h)] = rf[2 * j:2 * j + 2, span(h)].astype(BF)
        exchange(s6, r6, p6_s, p6_r, in_peer, h)

    for h in range(H):
        arrive(s6, r6, p6_s, p6_r, in_peer, h)
        for j in range(NZ):
            rg[2 * j:2 * j + 2, span(h)] = r6[j, :, span(h)].astype(F32)
        tot[:, span(h)] = tot[:, span(h)] + dot(weights, rg[:, span(h)].astype(BF), TN)
        for j in range(NX):
            s8[j, :, span(h)] = tot[j * T:(j + 1) * T, span(h)].astype(BF)
        for k in order:
            goal = mod(m + k, NX)
            send(rcopy(
                s8.at[goal, :, half(h)], r8.at[m, :, half(h)], p8_s.at[h, k], p8_r.at[h, k], at_x(goal)
            ))
    flush()
    for first in firsts:

        @pl.when(other_pair)
        def _(first=first):
            first.wait_send()

    for h in range(H):
        total = xg[m, :, span(h)].astype(F32) + s8[m, :, span(h)].astype(F32)
        for k in order:
            source = mod(m - k, NX)
            rcopy(
                s8.at[0, :, half(h)], r8.at[source, :, half(h)], p8_s.at[h, k], p8_r.at[h, k], at_x(source)
            ).wait_recv()
        for j in range(1, NX):
            total = total + r8[mod(m + j, NX), :, span(h)].astype(F32)
        out[:, span(h)] = total.astype(BF)


def body(NX, NY, NZ, *args):
    grad, routes, probs, dgp, dup, dwg, dwu, dwd, egp, eup, ewg, ewu, ewd = args
    T, D = grad.shape
    G = NX * T
    F = dwd.shape[0]
    SL = egp.shape[1]
    routes, probs = routes.T, probs.T
    egp, eup, ewg, ewu = [jnp.swapaxes(part, 1, 2) for part in (egp, eup, ewg, ewu)]
    RB = SL // NY
    DR = dwg.shape[0]
    DB = DR * NZ
    C = 4
    far = NX // 2
    V = pltpu.VMEM
    dma = pltpu.SemaphoreType.DMA
    scratch = [
        V((NX, T, D), BF), V((G, D), F32), V((G, D), BF), V((2, G), jnp.int32), V((2, G), BF),
        V((G, F), BF), V((G, F), BF), V((F, D), BF), V((F, SL), BF), V((F, SL), BF),
        V((F, D), BF), V((F, D), BF), V((F, D), BF),
        V((2, NZ, DR, F), BF), V((2, DB, F), F32), V((NY, 2, G, F), BF),
        V((NY, G, DB), BF), V((NY, G, DB), BF), V((RB, D), F32), V((RB, D), F32),
        V((NZ, 2, D), BF), V((NZ, 2, D), BF), V((NZ, 2, D), BF), V((NZ, 2, D), BF),
        V((NY, RB, D), BF), V((NY, RB, D), BF),
        V((2, far, RB, D), BF), V((2, far, RB, D), BF),
        V((NX, T, D), BF), V((NX, T, D), BF), V((G, D), F32),
        dma((12,)), dma((2, NX)), dma((2, NX)), dma((NZ,)), dma((NZ,)), dma((2,)),
        dma((NY,)), dma((NY,)), dma((NY,)), dma((NY,)),
        dma((2, NZ)), dma((2, NZ)), dma((2, NZ)), dma((2, NZ)),
        dma((2, far, C)), dma((2, far, C)), dma((2, far, C)), dma((2, far, C)),
        dma((2, NX)), dma((2, NX)),
    ]
    flops = 2 * 3 * F * D * (SL + G)
    return pl.pallas_call(
        functools.partial(kernel, NX, NY, NZ, C),
        out_shape=jax.ShapeDtypeStruct((T, D), BF),
        in_specs=[pl.BlockSpec(memory_space=pl.ANY)] * 13,
        out_specs=pl.BlockSpec(memory_space=pltpu.VMEM),
        scratch_shapes=scratch,
        compiler_params=pltpu.CompilerParams(
            collective_id=0, has_side_effects=True, vmem_limit_bytes=62 * 1024 * 1024
        ),
        cost_estimate=pl.CostEstimate(
            flops=flops, bytes_accessed=8 * F * D, transcendentals=F * (SL + G)
        ),
        name="layer_back",
    )(grad, routes, probs, dgp, dup, dwg, dwu, dwd, egp, eup, ewg, ewu, ewd)


def solution(mesh):
    NX = mesh.shape["tensor"]
    NE = mesh.shape["expert"]
    NY = NX
    NZ = NE // NY
    return jax.shard_map(
        functools.partial(body, NX, NY, NZ),
        mesh=mesh,
        in_specs=(
            P(("dp", "expert", "tensor"), None),
            P(("dp", "expert"), None),
            P(("dp", "expert"), None),
            P(("dp", "expert"), "tensor"),
            P(("dp", "expert"), "tensor"),
            P("expert", "tensor"),
            P("expert", "tensor"),
            P("tensor", None),
            P(("dp", "expert"), None, "tensor"),
            P(("dp", "expert"), None, "tensor"),
            P("expert", None, "tensor"),
            P("expert", None, "tensor"),
            P("expert", "tensor", None),
        ),
        out_specs=P(("dp", "expert", "tensor"), None),
        check_vma=False,
    )
```

```python
import functools
import math

import jax
import jax.numpy as jnp
from jax import lax
from jax.experimental import pallas as pl
from jax.experimental.pallas import tpu as pltpu
from jax.sharding import PartitionSpec as P

BF = jnp.bfloat16
F32 = jnp.float32
NT = (((1,), (1,)), ((), ()))
TN = (((0,), (0,)), ((), ()))
NN = (((1,), (0,)), ((), ()))


def mod(value, n):
    return lax.rem(value + 4 * n, n)


def dot(a, b, dims):
    return lax.dot_general(a, b, dims, preferred_element_type=F32)


def swiglu_back(upstream, gate_pre, up_pre):
    gate = gate_pre.astype(F32)
    up = up_pre.astype(F32)
    sigma = 1.0 / (1.0 + jnp.exp(-gate))
    grad_gate = upstream * up * (sigma * (1.0 + gate * (1.0 - sigma)))
    grad_up = upstream * (gate * sigma)
    return grad_gate, grad_up


def kernel(
    NX, NY, NZ,
    grad, routes, probs, dgp, dup, dwg, dwu, dwd, egp, eup, ewg, ewu, ewd,
    out,
    xg, xf, xb, rt, pr, dgp_v, dup_v, dwd_v, egp_v, eup_v, ewd_v, ewg_v, ewu_v,
    wg, wf, gg, do_s, do_r, rf, rg, fs, s2, r2, s6, r6, ag, bk, r_one, r_two, s8, r8, tot,
    ld_sem, p1_s, p1_r, wz_s, wz_r, sib, gg_s, gg_r, do_ss, do_rs,
    p2_s, p2_r, p6_s, p6_r, ag_s, ag_r, rs_s, rs_r, p8_s, p8_r,
):
    T, D = grad.shape
    G = NX * T
    F = dwd.shape[0]
    RB = ag.shape[2]
    Q = NX // 2
    DB = do_s.shape[2]
    DR = dwg.shape[0]
    SL = NY * RB

    dp = lax.axis_index("dp")
    ex = lax.axis_index("expert")
    m = lax.axis_index("tensor")
    y = ex // NZ
    z = ex % NZ

    def rcopy(src, dst, ss, rsem, device):
        return pltpu.make_async_remote_copy(
            src_ref=src, dst_ref=dst, send_sem=ss, recv_sem=rsem,
            device_id=device, device_id_type=pl.DeviceIdType.MESH,
        )

    def at_x(x):
        return (dp, ex, x)

    def at_yz(yy, zz):
        return (dp, yy * NZ + zz, m)

    sibling = (1 - dp, ex, m)
    own_pair = [mod(m + i * Q + z, NY) == 0 for i in range(2)]
    other_pair = [jnp.logical_not(own) for own in own_pair]

    barrier = pltpu.get_barrier_semaphore()

    def greet(device):
        pl.semaphore_signal(barrier, inc=1, device_id=device, device_id_type=pl.DeviceIdType.MESH)

    def out_peer(i, k):
        zz = mod(z + k, NZ)
        return at_yz(mod(y + m + i * Q + zz, NY), zz)

    def in_peer(i, k):
        return at_yz(mod(y - m - i * Q - z, NY), mod(z + k, NZ))

    for k in range(1, NX):
        greet(at_x(mod(m + k, NX)))
    for i in range(2):
        for k in range(1, NZ):
            greet(in_peer(i, k))
            greet(out_peer(i, k))

        @pl.when(other_pair[i])
        def _(i=i):
            greet(in_peer(i, 0))
            greet(out_peer(i, 0))

    for k in range(1, NZ):
        greet(at_yz(y, mod(z + k, NZ)))
    for k in range(1, NY):
        greet(at_yz(mod(y + k, NY), z))
    greet(sibling)

    loads = [
        pltpu.make_async_copy(grad, xg.at[m], ld_sem.at[0]),
        pltpu.make_async_copy(routes, rt, ld_sem.at[1]),
        pltpu.make_async_copy(probs, pr, ld_sem.at[2]),
        pltpu.make_async_copy(dwd, dwd_v, ld_sem.at[3]),
        pltpu.make_async_copy(dgp, dgp_v, ld_sem.at[4]),
        pltpu.make_async_copy(dup, dup_v, ld_sem.at[5]),
        pltpu.make_async_copy(ewd.at[0], ewd_v, ld_sem.at[6]),
        pltpu.make_async_copy(egp.at[0], egp_v, ld_sem.at[7]),
        pltpu.make_async_copy(eup.at[0], eup_v, ld_sem.at[8]),
        pltpu.make_async_copy(ewg.at[0], ewg_v, ld_sem.at[9]),
        pltpu.make_async_copy(ewu.at[0], ewu_v, ld_sem.at[10]),
    ]
    own_gate = pltpu.make_async_copy(dwg, wg.at[0, z], ld_sem.at[11])
    own_up = pltpu.make_async_copy(dwu, wg.at[1, z], ld_sem.at[11])
    for load in loads[:3]:
        load.start()

    @pl.when(dp == 0)
    def _():
        own_gate.start()

    @pl.when(dp == 1)
    def _():
        own_up.start()

    for load in loads[3:]:
        load.start()

    fixed = NX - 1 + NY - 1 + NZ - 1 + 1 + 4 * (NZ - 1)
    others = other_pair[0].astype(jnp.int32) + other_pair[1].astype(jnp.int32)
    pl.semaphore_wait(barrier, fixed + 2 * others)

    sent = []

    def send(copy):
        copy.start()
        sent.append(copy)

    def flush():
        for copy in sent:
            copy.wait_send()
        sent.clear()

    H = 2
    HW = D // H

    def half(h):
        return pl.ds(h * HW, HW)

    def span(h):
        return slice(h * HW, (h + 1) * HW)

    order = sorted(range(1, NX), key=lambda k: -min(k, NX - k))

    def gather(h):
        for k in order:
            send(rcopy(
                grad.at[:, half(h)], xg.at[m, :, half(h)], p1_s.at[h, k], p1_r.at[h, k], at_x(mod(m + k, NX))
            ))

    gather(0)

    loads[1].wait()
    loads[2].wait()
    slot = lax.broadcasted_iota(jnp.int32, (2 * RB, G), 0)
    owner = (slot >= RB).astype(jnp.int32)
    zc = lax.shift_right_logical(slot - owner * RB, 1)
    named = jnp.bitwise_and(y + m + owner * Q + zc, NY - 1) * NZ + zc
    r0 = rt[0:1, :]
    r1 = rt[1:2, :]
    hit0 = (r0 == named).astype(F32)
    hit1 = (r1 == named).astype(F32)
    hits = hit0 + hit1
    earlier = (
        lax.broadcasted_iota(jnp.int32, (G, G), 0) < lax.broadcasted_iota(jnp.int32, (G, G), 1)
    ).astype(BF)
    rank = dot(hits.astype(BF), earlier, NN)
    taken = (rank == jnp.bitwise_and(slot, 1).astype(F32)).astype(F32)
    select = (hits * taken).astype(BF)
    pv = pr[...].astype(F32)
    weights = ((hit0 * pv[0:1, :] + hit1 * pv[1:2, :]) * taken).astype(BF)

    flush()
    gather(1)

    pltpu.make_async_copy(dwg, wg.at[0, z], ld_sem.at[11]).wait()
    for k in range(1, NZ):
        send(rcopy(wg.at[dp, z], wg.at[dp, z], wz_s.at[k], wz_r.at[k], at_yz(y, mod(z + k, NZ))))

    firsts = []

    def exchange(src, dst, ssem, rsem, peer, h):
        for i in range(2):
            local = pltpu.make_async_copy(src.at[i, z, :, half(h)], dst.at[i, z, :, half(h)], rsem.at[h, i, 0])

            @pl.when(own_pair[i])
            def _(local=local):
                local.start()

            first = rcopy(
                src.at[i, z, :, half(h)], dst.at[i, z, :, half(h)], ssem.at[h, i, 0], rsem.at[h, i, 0], peer(i, 0)
            )

            @pl.when(other_pair[i])
            def _(first=first):
                first.start()

            firsts.append((i, first))
            for k in range(1, NZ):
                send(rcopy(
                    src.at[i, mod(z + k, NZ), :, half(h)], dst.at[i, z, :, half(h)],
                    ssem.at[h, i, k], rsem.at[h, i, k], peer(i, k),
                ))

    def arrive(src, dst, ssem, rsem, peer, h):
        for i in range(2):
            for k in range(NZ):
                rcopy(
                    src.at[i, 0, :, half(h)], dst.at[i, mod(z - k, NZ), :, half(h)],
                    ssem.at[h, i, k], rsem.at[h, i, k], peer(i, k),
                ).wait_recv()

    def split_rows(rows, parts, h):
        for i in range(2):
            for j in range(NZ):
                low = i * RB + 2 * j
                parts[i, j, :, span(h)] = rows[low:low + 2, span(h)].astype(BF)

    def join_rows(rows, parts, h):
        for i in range(2):
            for j in range(NZ):
                low = i * RB + 2 * j
                rows[low:low + 2, span(h)] = parts[i, j, :, span(h)].astype(F32)

    loads[0].wait()
    for h in range(H):
        for k in order:
            source = mod(m - k, NX)
            rcopy(
                grad.at[:, half(h)], xg.at[source, :, half(h)], p1_s.at[h, k], p1_r.at[h, k], at_x(source)
            ).wait_recv()
        for j in range(NX):
            xf[j * T:(j + 1) * T, span(h)] = xg[j, :, span(h)].astype(F32)
        xb[:, span(h)] = xf[:, span(h)].astype(BF)
        rf[:, span(h)] = dot(select, xb[:, span(h)], NN)
        split_rows(rf, s2, h)
        exchange(s2, r2, p2_s, p2_r, out_peer, h)

    def block_of(member):
        return mod(y - z - member, NY)

    def slab(member):
        return block_of(member) % Q

    def side(member):
        return block_of(member) // Q

    loads[3].wait()
    loads[4].wait()
    loads[5].wait()
    dense_up = jnp.transpose(dot(dwd_v[...], xb[...], NT))
    dense_gg, dense_gu = swiglu_back(dense_up, dgp_v[...], dup_v[...])
    gg[y, 0] = dense_gg.astype(BF)
    gg[y, 1] = dense_gu.astype(BF)

    steps = [2, -2, 1, -1]

    def ag_copy(n, h, origin, goal):
        if n < 2:
            ref = ag.at[slab(origin), side(origin), :, half(h)]
        else:
            ref = ag.at[slab(origin), :, :, half(h)]
        return rcopy(ref, ref, ag_s.at[h, n], ag_r.at[h, n], at_x(mod(goal, NX)))

    for h in range(H):
        arrive(s2, r2, p2_s, p2_r, out_peer, h)
        join_rows(rg, r2, h)
        ag[slab(m), side(m), :, span(h)] = rg[0:RB, span(h)].astype(BF)
        ag[slab(m), 1 - side(m), :, span(h)] = rg[RB:2 * RB, span(h)].astype(BF)
        for n, step in enumerate(steps):
            send(ag_copy(n, h, m, m + step))

    for k in range(1, NY):
        send(rcopy(gg.at[y], gg.at[y], gg_s.at[k], gg_r.at[k], at_yz(mod(y + k, NY), z)))
    for k in range(1, NZ):
        rcopy(
            wg.at[dp, z], wg.at[dp, mod(z - k, NZ)], wz_s.at[k], wz_r.at[k], at_yz(y, mod(z + k, NZ))
        ).wait_recv()
    send(rcopy(wg.at[dp], wg.at[dp], sib.at[0], sib.at[1], sibling))

    loads[6].wait()
    upstream = jnp.zeros((F, SL), F32)
    for h in range(H):
        for n, step in enumerate(steps):
            ag_copy(n, h, m - step, m + step).wait_recv()
        rows = jnp.concatenate([ag[b % Q, b // Q, :, span(h)] for b in range(NY)], axis=0)
        upstream = upstream + dot(ewd_v[:, span(h)], rows, NT)
    loads[7].wait()
    loads[8].wait()
    expert_gg, expert_gu = [
        jnp.transpose(part).astype(BF) for part in swiglu_back(upstream, egp_v[...], eup_v[...])
    ]

    def rs_copy(n, h):
        goal = m + steps[n]
        if n < 2:
            src = bk.at[slab(goal), side(goal), :, half(h)]
            dst = r_two.at[n, :, half(h)]
        else:
            src = bk.at[slab(goal), :, :, half(h)]
            dst = r_one.at[n - 2, :, :, half(h)]
        return rcopy(src, dst, rs_s.at[h, n], rs_r.at[h, n], at_x(mod(goal, NX)))

    def back(h):
        rows = dot(expert_gg, ewg_v[:, span(h)], NN) + dot(expert_gu, ewu_v[:, span(h)], NN)
        rows = rows.astype(BF)
        for b in range(NY):
            bk[b % Q, b // Q, :, span(h)] = rows[b * RB:(b + 1) * RB]

    loads[9].wait()
    loads[10].wait()
    back(0)
    for n in range(4):
        send(rs_copy(n, 0))
    back(1)

    for k in range(1, NY):
        rcopy(
            gg.at[y], gg.at[mod(y - k, NY)], gg_s.at[k], gg_r.at[k], at_yz(mod(y + k, NY), z)
        ).wait_recv()
    rcopy(wg.at[1 - dp], wg.at[1 - dp], sib.at[0], sib.at[1], sibling).wait_recv()
    dense = jnp.zeros((NY * G, DB), F32)
    for which in range(2):
        for j in range(NZ):
            wf[which, j * DR:(j + 1) * DR, :] = wg[which, j].astype(F32)
        dense = dense + dot(gg[:, which].reshape(NY * G, F), wf[which].astype(BF), NT)
    do_s[...] = dense.astype(BF).reshape(NY, G, DB)
    for n in range(4):
        send(rs_copy(n, 1))
    for k in range(1, NY):
        goal = mod(y + k, NY)
        send(rcopy(do_s.at[goal], do_r.at[y], do_ss.at[k], do_rs.at[k], at_yz(goal, z)))
    do_r[y] = do_s[y]

    for h in range(H):
        for n in range(4):
            rs_copy(n, h).wait_recv()
        fs[:, :, span(h)] = (
            bk[slab(m), :, :, span(h)].astype(F32)
            + r_one[0, :, :, span(h)].astype(F32)
            + r_one[1, :, :, span(h)].astype(F32)
        )
        rf[0:RB, span(h)] = (
            fs[side(m), :, span(h)] + r_two[0, :, span(h)].astype(F32) + r_two[1, :, span(h)].astype(F32)
        )
        rf[RB:2 * RB, span(h)] = fs[1 - side(m), :, span(h)]
        split_rows(rf, s6, h)
        exchange(s6, r6, p6_s, p6_r, in_peer, h)

    for k in range(1, NY):
        rcopy(
            do_s.at[y], do_r.at[mod(y - k, NY)], do_ss.at[k], do_rs.at[k], at_yz(mod(y + k, NY), z)
        ).wait_recv()
    pair = 2 if (2 * DB) % 128 == 0 and NY % 2 == 0 else NY
    for j in range(0, NY, pair):
        tot[:, j * DB:(j + pair) * DB] = jnp.concatenate(
            [do_r[j + i].astype(F32) for i in range(pair)], axis=1
        )

    for h in range(H):
        arrive(s6, r6, p6_s, p6_r, in_peer, h)
        join_rows(rg, r6, h)
        tot[:, span(h)] = tot[:, span(h)] + dot(weights, rg[:, span(h)].astype(BF), TN)
        for j in range(NX):
            s8[j, :, span(h)] = tot[j * T:(j + 1) * T, span(h)].astype(BF)
        for k in order:
            goal = mod(m + k, NX)
            send(rcopy(
                s8.at[goal, :, half(h)], r8.at[m, :, half(h)], p8_s.at[h, k], p8_r.at[h, k], at_x(goal)
            ))
    flush()
    for i, first in firsts:

        @pl.when(other_pair[i])
        def _(first=first):
            first.wait_send()

    for h in range(H):
        total = xg[m, :, span(h)].astype(F32) + s8[m, :, span(h)].astype(F32)
        for k in order:
            source = mod(m - k, NX)
            rcopy(
                s8.at[0, :, half(h)], r8.at[source, :, half(h)], p8_s.at[h, k], p8_r.at[h, k], at_x(source)
            ).wait_recv()
        for j in range(1, NX):
            total = total + r8[mod(m + j, NX), :, span(h)].astype(F32)
        out[:, span(h)] = total.astype(BF)


def body(NX, NY, NZ, *args):
    grad, routes, probs, dgp, dup, dwg, dwu, dwd, egp, eup, ewg, ewu, ewd = args
    T, D = grad.shape
    G = NX * T
    F = dwd.shape[0]
    SL = egp.shape[1]
    routes, probs = routes.T, probs.T
    egp, eup, ewg, ewu = [jnp.swapaxes(part, 1, 2) for part in (egp, eup, ewg, ewu)]
    RB = SL // NY
    DR = dwg.shape[0]
    DB = DR * NZ
    Q = NX // 2
    V = pltpu.VMEM
    dma = pltpu.SemaphoreType.DMA
    scratch = [
        V((NX, T, D), BF), V((G, D), F32), V((G, D), BF), V((2, G), jnp.int32), V((2, G), BF),
        V((G, F), BF), V((G, F), BF), V((F, D), BF), V((F, SL), BF), V((F, SL), BF),
        V((F, D), BF), V((F, D), BF), V((F, D), BF),
        V((2, NZ, DR, F), BF), V((2, DB, F), F32), V((NY, 2, G, F), BF),
        V((NY, G, DB), BF), V((NY, G, DB), BF), V((2 * RB, D), F32), V((2 * RB, D), F32), V((2, RB, D), F32),
        V((2, NZ, 2, D), BF), V((2, NZ, 2, D), BF), V((2, NZ, 2, D), BF), V((2, NZ, 2, D), BF),
        V((Q, 2, RB, D), BF), V((Q, 2, RB, D), BF), V((2, 2, RB, D), BF), V((2, RB, D), BF),
        V((NX, T, D), BF), V((NX, T, D), BF), V((G, D), F32),
        dma((12,)), dma((2, NX)), dma((2, NX)), dma((NZ,)), dma((NZ,)), dma((2,)),
        dma((NY,)), dma((NY,)), dma((NY,)), dma((NY,)),
        dma((2, 2, NZ)), dma((2, 2, NZ)), dma((2, 2, NZ)), dma((2, 2, NZ)),
        dma((2, 4)), dma((2, 4)), dma((2, 4)), dma((2, 4)),
        dma((2, NX)), dma((2, NX)),
    ]
    flops = 2 * 3 * F * D * (SL + G)
    return pl.pallas_call(
        functools.partial(kernel, NX, NY, NZ),
        out_shape=jax.ShapeDtypeStruct((T, D), BF),
        in_specs=[pl.BlockSpec(memory_space=pl.ANY)] * 13,
        out_specs=pl.BlockSpec(memory_space=pltpu.VMEM),
        scratch_shapes=scratch,
        compiler_params=pltpu.CompilerParams(
            collective_id=0, has_side_effects=True, vmem_limit_bytes=62 * 1024 * 1024
        ),
        cost_estimate=pl.CostEstimate(
            flops=flops, bytes_accessed=8 * F * D, transcendentals=F * (SL + G)
        ),
        name="layer_back",
    )(grad, routes, probs, dgp, dup, dwg, dwu, dwd, egp, eup, ewg, ewu, ewd)


def solution(mesh):
    NX = mesh.shape["tensor"]
    NE = mesh.shape["expert"]
    NY = NX
    NZ = NE // NY
    return jax.shard_map(
        functools.partial(body, NX, NY, NZ),
        mesh=mesh,
        in_specs=(
            P(("dp", "expert", "tensor"), None),
            P(("dp", "expert"), None),
            P(("dp", "expert"), None),
            P(("dp", "expert"), "tensor"),
            P(("dp", "expert"), "tensor"),
            P("expert", "tensor"),
            P("expert", "tensor"),
            P("tensor", None),
            P(("dp", "expert"), None, "tensor"),
            P(("dp", "expert"), None, "tensor"),
            P("expert", None, "tensor"),
            P("expert", None, "tensor"),
            P("expert", "tensor", None),
        ),
        out_specs=P(("dp", "expert", "tensor"), None),
        check_vma=False,
    )
```

```python
import functools
import math

import jax
import jax.numpy as jnp
from jax import lax
from jax.experimental import pallas as pl
from jax.experimental.pallas import tpu as pltpu
from jax.sharding import PartitionSpec as P

BF = jnp.bfloat16
F32 = jnp.float32
NT = (((1,), (1,)), ((), ()))
TN = (((0,), (0,)), ((), ()))
NN = (((1,), (0,)), ((), ()))


def mod(value, n):
    return lax.rem(value + 4 * n, n)


def dot(a, b, dims):
    return lax.dot_general(a, b, dims, preferred_element_type=F32)


def swiglu_back(upstream, gate_pre, up_pre):
    gate = gate_pre.astype(F32)
    up = up_pre.astype(F32)
    sigma = 1.0 / (1.0 + jnp.exp(-gate))
    grad_gate = upstream * up * (sigma * (1.0 + gate * (1.0 - sigma)))
    grad_up = upstream * (gate * sigma)
    return grad_gate, grad_up


def kernel(
    NX, NY, NZ,
    grad, routes, probs, dgp, dup, dwg, dwu, dwd, egp, eup, ewg, ewu, ewd,
    out,
    xg, xf, xb, rt, pr, dgp_v, dup_v, dwd_v, egp_v, eup_v, ewd_v, ewg_v, ewu_v,
    wg, wf, gg, do_s, do_r, rf, rg, fs, s2, r2, s6, r6, ag, bk, r_one, r_two, s8, r8, tot,
    ld_sem, p1_s, p1_r, wz_s, wz_r, sib, gg_s, gg_r, do_ss, do_rs,
    p2_s, p2_r, p6_s, p6_r, ag_s, ag_r, rs_s, rs_r, p8_s, p8_r,
):
    T, D = grad.shape
    G = NX * T
    F = dwd.shape[0]
    RB = ag.shape[2]
    Q = NX // 2
    DB = do_s.shape[2]
    DR = dwg.shape[0]
    SL = NY * RB

    dp = lax.axis_index("dp")
    ex = lax.axis_index("expert")
    m = lax.axis_index("tensor")
    y = ex // NZ
    z = ex % NZ

    def rcopy(src, dst, ss, rsem, device):
        return pltpu.make_async_remote_copy(
            src_ref=src, dst_ref=dst, send_sem=ss, recv_sem=rsem,
            device_id=device, device_id_type=pl.DeviceIdType.MESH,
        )

    def at_x(x):
        return (dp, ex, x)

    def at_yz(yy, zz):
        return (dp, yy * NZ + zz, m)

    sibling = (1 - dp, ex, m)
    own_pair = [mod(m + i * Q + z, NY) == 0 for i in range(2)]
    other_pair = [jnp.logical_not(own) for own in own_pair]

    barrier = pltpu.get_barrier_semaphore()

    def greet(device):
        pl.semaphore_signal(barrier, inc=1, device_id=device, device_id_type=pl.DeviceIdType.MESH)

    def out_peer(i, k):
        zz = mod(z + k, NZ)
        return at_yz(mod(y + m + i * Q + zz, NY), zz)

    def in_peer(i, k):
        return at_yz(mod(y - m - i * Q - z, NY), mod(z + k, NZ))

    for k in range(1, NX):
        greet(at_x(mod(m + k, NX)))
    for i in range(2):
        for k in range(1, NZ):
            greet(in_peer(i, k))
            greet(out_peer(i, k))

        @pl.when(other_pair[i])
        def _(i=i):
            greet(in_peer(i, 0))
            greet(out_peer(i, 0))

    for k in range(1, NZ):
        greet(at_yz(y, mod(z + k, NZ)))
    for k in range(1, NY):
        greet(at_yz(mod(y + k, NY), z))
    greet(sibling)

    loads = [
        pltpu.make_async_copy(grad, xg.at[m], ld_sem.at[0]),
        pltpu.make_async_copy(routes, rt, ld_sem.at[1]),
        pltpu.make_async_copy(probs, pr, ld_sem.at[2]),
        pltpu.make_async_copy(dwd, dwd_v, ld_sem.at[3]),
        pltpu.make_async_copy(dgp, dgp_v, ld_sem.at[4]),
        pltpu.make_async_copy(dup, dup_v, ld_sem.at[5]),
        pltpu.make_async_copy(ewd.at[0], ewd_v, ld_sem.at[6]),
        pltpu.make_async_copy(egp.at[0], egp_v, ld_sem.at[7]),
        pltpu.make_async_copy(eup.at[0], eup_v, ld_sem.at[8]),
        pltpu.make_async_copy(ewg.at[0], ewg_v, ld_sem.at[9]),
        pltpu.make_async_copy(ewu.at[0], ewu_v, ld_sem.at[10]),
    ]
    own_gate = pltpu.make_async_copy(dwg, wg.at[0, z], ld_sem.at[11])
    own_up = pltpu.make_async_copy(dwu, wg.at[1, z], ld_sem.at[11])
    for load in loads[:3]:
        load.start()

    @pl.when(dp == 0)
    def _():
        own_gate.start()

    @pl.when(dp == 1)
    def _():
        own_up.start()

    for load in loads[3:]:
        load.start()

    fixed = NX - 1 + NY - 1 + NZ - 1 + 1 + 4 * (NZ - 1)
    others = other_pair[0].astype(jnp.int32) + other_pair[1].astype(jnp.int32)
    pl.semaphore_wait(barrier, fixed + 2 * others)

    sent = []

    def send(copy):
        copy.start()
        sent.append(copy)

    def flush():
        for copy in sent:
            copy.wait_send()
        sent.clear()

    H = HALVES
    HW = D // H

    def half(h):
        return pl.ds(h * HW, HW)

    def span(h):
        return slice(h * HW, (h + 1) * HW)

    order = sorted(range(1, NX), key=lambda k: -min(k, NX - k))

    def gather(h):
        for k in order:
            send(rcopy(
                grad.at[:, half(h)], xg.at[m, :, half(h)], p1_s.at[h, k], p1_r.at[h, k], at_x(mod(m + k, NX))
            ))

    for h in range(H):
        gather(h)

    loads[1].wait()
    loads[2].wait()
    slot = lax.broadcasted_iota(jnp.int32, (2 * RB, G), 0)
    owner = (slot >= RB).astype(jnp.int32)
    zc = lax.shift_right_logical(slot - owner * RB, 1)
    named = jnp.bitwise_and(y + m + owner * Q + zc, NY - 1) * NZ + zc
    r0 = rt[0:1, :]
    r1 = rt[1:2, :]
    hit0 = (r0 == named).astype(F32)
    hit1 = (r1 == named).astype(F32)
    hits = hit0 + hit1
    earlier = (
        lax.broadcasted_iota(jnp.int32, (G, G), 0) < lax.broadcasted_iota(jnp.int32, (G, G), 1)
    ).astype(BF)
    rank = dot(hits.astype(BF), earlier, NN)
    taken = (rank == jnp.bitwise_and(slot, 1).astype(F32)).astype(F32)
    select = (hits * taken).astype(BF)
    pv = pr[...].astype(F32)
    weights = ((hit0 * pv[0:1, :] + hit1 * pv[1:2, :]) * taken).astype(BF)


    firsts = []

    def exchange(src, dst, ssem, rsem, peer, h):
        for i in range(2):
            local = pltpu.make_async_copy(src.at[i, z, :, half(h)], dst.at[i, z, :, half(h)], rsem.at[h, i, 0])

            @pl.when(own_pair[i])
            def _(local=local):
                local.start()

            first = rcopy(
                src.at[i, z, :, half(h)], dst.at[i, z, :, half(h)], ssem.at[h, i, 0], rsem.at[h, i, 0], peer(i, 0)
            )

            @pl.when(other_pair[i])
            def _(first=first):
                first.start()

            firsts.append((i, first))
            for k in sorted(range(1, NZ), key=lambda k: -min(k, NZ - k)):
                send(rcopy(
                    src.at[i, mod(z + k, NZ), :, half(h)], dst.at[i, z, :, half(h)],
                    ssem.at[h, i, k], rsem.at[h, i, k], peer(i, k),
                ))

    def arrive(src, dst, ssem, rsem, peer, h):
        for i in range(2):
            for k in range(NZ):
                rcopy(
                    src.at[i, 0, :, half(h)], dst.at[i, mod(z - k, NZ), :, half(h)],
                    ssem.at[h, i, k], rsem.at[h, i, k], peer(i, k),
                ).wait_recv()

    def split_rows(rows, parts, h):
        for i in range(2):
            for j in range(NZ):
                low = i * RB + 2 * j
                parts[i, j, :, span(h)] = rows[low:low + 2, span(h)].astype(BF)

    def join_rows(rows, parts, h):
        for i in range(2):
            for j in range(NZ):
                low = i * RB + 2 * j
                rows[low:low + 2, span(h)] = parts[i, j, :, span(h)].astype(F32)

    loads[0].wait()
    for h in range(H):
        for k in order:
            source = mod(m - k, NX)
            rcopy(
                grad.at[:, half(h)], xg.at[source, :, half(h)], p1_s.at[h, k], p1_r.at[h, k], at_x(source)
            ).wait_recv()
        for j in range(NX):
            xf[j * T:(j + 1) * T, span(h)] = xg[j, :, span(h)].astype(F32)
        xb[:, span(h)] = xf[:, span(h)].astype(BF)
        rf[:, span(h)] = dot(select, xb[:, span(h)], NN)
        split_rows(rf, s2, h)
        exchange(s2, r2, p2_s, p2_r, out_peer, h)

    def block_of(member):
        return mod(y - z - member, NY)

    def slab(member):
        return block_of(member) % Q

    def side(member):
        return block_of(member) // Q

    loads[3].wait()
    loads[4].wait()
    loads[5].wait()
    dense_up = jnp.transpose(dot(dwd_v[...], xb[...], NT))
    dense_gg, dense_gu = swiglu_back(dense_up, dgp_v[...], dup_v[...])
    gg[y, 0] = dense_gg.astype(BF)
    gg[y, 1] = dense_gu.astype(BF)

    steps = [2, -2, 1, -1]

    def ag_copy(n, h, origin, goal):
        if n < 2:
            ref = ag.at[slab(origin), side(origin), :, half(h)]
        else:
            ref = ag.at[slab(origin), :, :, half(h)]
        return rcopy(ref, ref, ag_s.at[h, n], ag_r.at[h, n], at_x(mod(goal, NX)))

    for h in range(H):
        arrive(s2, r2, p2_s, p2_r, out_peer, h)
        join_rows(rg, r2, h)
        ag[slab(m), side(m), :, span(h)] = rg[0:RB, span(h)].astype(BF)
        ag[slab(m), 1 - side(m), :, span(h)] = rg[RB:2 * RB, span(h)].astype(BF)
        for n, step in enumerate(steps):
            send(ag_copy(n, h, m, m + step))

    pltpu.make_async_copy(dwg, wg.at[0, z], ld_sem.at[11]).wait()
    for k in range(1, NZ):
        send(rcopy(wg.at[dp, z], wg.at[dp, z], wz_s.at[k], wz_r.at[k], at_yz(y, mod(z + k, NZ))))
    for k in range(1, NY):
        send(rcopy(gg.at[y], gg.at[y], gg_s.at[k], gg_r.at[k], at_yz(mod(y + k, NY), z)))

    loads[6].wait()
    upstream = jnp.zeros((F, SL), F32)
    for h in range(H):
        for n, step in enumerate(steps):
            ag_copy(n, h, m - step, m + step).wait_recv()
        rows = jnp.concatenate([ag[b % Q, b // Q, :, span(h)] for b in range(NY)], axis=0)
        upstream = upstream + dot(ewd_v[:, span(h)], rows, NT)
    loads[7].wait()
    loads[8].wait()
    expert_gg, expert_gu = [
        jnp.transpose(part).astype(BF) for part in swiglu_back(upstream, egp_v[...], eup_v[...])
    ]

    def rs_copy(n, h):
        goal = m + steps[n]
        if n < 2:
            src = bk.at[slab(goal), side(goal), :, half(h)]
            dst = r_two.at[n, :, half(h)]
        else:
            src = bk.at[slab(goal), :, :, half(h)]
            dst = r_one.at[n - 2, :, :, half(h)]
        return rcopy(src, dst, rs_s.at[h, n], rs_r.at[h, n], at_x(mod(goal, NX)))

    def back(h):
        rows = dot(expert_gg, ewg_v[:, span(h)], NN) + dot(expert_gu, ewu_v[:, span(h)], NN)
        rows = rows.astype(BF)
        for b in range(NY):
            bk[b % Q, b // Q, :, span(h)] = rows[b * RB:(b + 1) * RB]

    loads[9].wait()
    loads[10].wait()
    for h in range(H):
        back(h)
        for n in range(4):
            send(rs_copy(n, h))

    for k in range(1, NZ):
        rcopy(
            wg.at[dp, z], wg.at[dp, mod(z - k, NZ)], wz_s.at[k], wz_r.at[k], at_yz(y, mod(z + k, NZ))
        ).wait_recv()
    send(rcopy(wg.at[dp], wg.at[dp], sib.at[0], sib.at[1], sibling))

    for k in range(1, NY):
        rcopy(
            gg.at[y], gg.at[mod(y - k, NY)], gg_s.at[k], gg_r.at[k], at_yz(mod(y + k, NY), z)
        ).wait_recv()
    rcopy(wg.at[1 - dp], wg.at[1 - dp], sib.at[0], sib.at[1], sibling).wait_recv()
    dense = jnp.zeros((NY * G, DB), F32)
    for which in range(2):
        for j in range(NZ):
            wf[which, j * DR:(j + 1) * DR, :] = wg[which, j].astype(F32)
        dense = dense + dot(gg[:, which].reshape(NY * G, F), wf[which].astype(BF), NT)
    do_s[...] = dense.astype(BF).reshape(NY, G, DB)
    for k in range(1, NY):
        goal = mod(y + k, NY)
        send(rcopy(do_s.at[goal], do_r.at[y], do_ss.at[k], do_rs.at[k], at_yz(goal, z)))
    do_r[y] = do_s[y]

    for h in range(H):
        for n in range(4):
            rs_copy(n, h).wait_recv()
        fs[:, :, span(h)] = (
            bk[slab(m), :, :, span(h)].astype(F32)
            + r_one[0, :, :, span(h)].astype(F32)
            + r_one[1, :, :, span(h)].astype(F32)
        )
        rf[0:RB, span(h)] = (
            fs[side(m), :, span(h)] + r_two[0, :, span(h)].astype(F32) + r_two[1, :, span(h)].astype(F32)
        )
        rf[RB:2 * RB, span(h)] = fs[1 - side(m), :, span(h)]
        split_rows(rf, s6, h)
        exchange(s6, r6, p6_s, p6_r, in_peer, h)

    for k in range(1, NY):
        rcopy(
            do_s.at[y], do_r.at[mod(y - k, NY)], do_ss.at[k], do_rs.at[k], at_yz(mod(y + k, NY), z)
        ).wait_recv()
    pair = 2 if (2 * DB) % 128 == 0 and NY % 2 == 0 else NY
    for j in range(0, NY, pair):
        tot[:, j * DB:(j + pair) * DB] = jnp.concatenate(
            [do_r[j + i].astype(F32) for i in range(pair)], axis=1
        )

    for h in range(H):
        arrive(s6, r6, p6_s, p6_r, in_peer, h)
        join_rows(rg, r6, h)
        tot[:, span(h)] = tot[:, span(h)] + dot(weights, rg[:, span(h)].astype(BF), TN)
        for j in range(NX):
            s8[j, :, span(h)] = tot[j * T:(j + 1) * T, span(h)].astype(BF)
        for k in order:
            goal = mod(m + k, NX)
            send(rcopy(
                s8.at[goal, :, half(h)], r8.at[m, :, half(h)], p8_s.at[h, k], p8_r.at[h, k], at_x(goal)
            ))
    flush()
    for i, first in firsts:

        @pl.when(other_pair[i])
        def _(first=first):
            first.wait_send()

    for h in range(H):
        total = xg[m, :, span(h)].astype(F32) + s8[m, :, span(h)].astype(F32)
        for k in order:
            source = mod(m - k, NX)
            rcopy(
                s8.at[0, :, half(h)], r8.at[source, :, half(h)], p8_s.at[h, k], p8_r.at[h, k], at_x(source)
            ).wait_recv()
        for j in range(1, NX):
            total = total + r8[mod(m + j, NX), :, span(h)].astype(F32)
        out[:, span(h)] = total.astype(BF)


HALVES = 2


def body(NX, NY, NZ, *args):
    grad, routes, probs, dgp, dup, dwg, dwu, dwd, egp, eup, ewg, ewu, ewd = args
    T, D = grad.shape
    G = NX * T
    F = dwd.shape[0]
    SL = egp.shape[1]
    routes, probs = routes.T, probs.T
    egp, eup, ewg, ewu = [jnp.swapaxes(part, 1, 2) for part in (egp, eup, ewg, ewu)]
    RB = SL // NY
    DR = dwg.shape[0]
    DB = DR * NZ
    Q = NX // 2
    V = pltpu.VMEM
    dma = pltpu.SemaphoreType.DMA
    scratch = [
        V((NX, T, D), BF), V((G, D), F32), V((G, D), BF), V((2, G), jnp.int32), V((2, G), BF),
        V((G, F), BF), V((G, F), BF), V((F, D), BF), V((F, SL), BF), V((F, SL), BF),
        V((F, D), BF), V((F, D), BF), V((F, D), BF),
        V((2, NZ, DR, F), BF), V((2, DB, F), F32), V((NY, 2, G, F), BF),
        V((NY, G, DB), BF), V((NY, G, DB), BF), V((2 * RB, D), F32), V((2 * RB, D), F32), V((2, RB, D), F32),
        V((2, NZ, 2, D), BF), V((2, NZ, 2, D), BF), V((2, NZ, 2, D), BF), V((2, NZ, 2, D), BF),
        V((Q, 2, RB, D), BF), V((Q, 2, RB, D), BF), V((2, 2, RB, D), BF), V((2, RB, D), BF),
        V((NX, T, D), BF), V((NX, T, D), BF), V((G, D), F32),
        dma((12,)), dma((HALVES, NX)), dma((HALVES, NX)), dma((NZ,)), dma((NZ,)), dma((2,)),
        dma((NY,)), dma((NY,)), dma((NY,)), dma((NY,)),
        dma((HALVES, 2, NZ)), dma((HALVES, 2, NZ)), dma((HALVES, 2, NZ)), dma((HALVES, 2, NZ)),
        dma((HALVES, 4)), dma((HALVES, 4)), dma((HALVES, 4)), dma((HALVES, 4)),
        dma((HALVES, NX)), dma((HALVES, NX)),
    ]
    flops = 2 * 3 * F * D * (SL + G)
    return pl.pallas_call(
        functools.partial(kernel, NX, NY, NZ),
        out_shape=jax.ShapeDtypeStruct((T, D), BF),
        in_specs=[pl.BlockSpec(memory_space=pl.ANY)] * 13,
        out_specs=pl.BlockSpec(memory_space=pltpu.VMEM),
        scratch_shapes=scratch,
        compiler_params=pltpu.CompilerParams(
            collective_id=0, has_side_effects=True, vmem_limit_bytes=62 * 1024 * 1024
        ),
        cost_estimate=pl.CostEstimate(
            flops=flops, bytes_accessed=8 * F * D, transcendentals=F * (SL + G)
        ),
        name="layer_back",
    )(grad, routes, probs, dgp, dup, dwg, dwu, dwd, egp, eup, ewg, ewu, ewd)


def solution(mesh):
    NX = mesh.shape["tensor"]
    NE = mesh.shape["expert"]
    NY = NX
    NZ = NE // NY
    return jax.shard_map(
        functools.partial(body, NX, NY, NZ),
        mesh=mesh,
        in_specs=(
            P(("dp", "expert", "tensor"), None),
            P(("dp", "expert"), None),
            P(("dp", "expert"), None),
            P(("dp", "expert"), "tensor"),
            P(("dp", "expert"), "tensor"),
            P("expert", "tensor"),
            P("expert", "tensor"),
            P("tensor", None),
            P(("dp", "expert"), None, "tensor"),
            P(("dp", "expert"), None, "tensor"),
            P("expert", None, "tensor"),
            P("expert", None, "tensor"),
            P("expert", "tensor", None),
        ),
        out_specs=P(("dp", "expert", "tensor"), None),
        check_vma=False,
    )
```
